256 devices in a mesh: band: 16 (over y, z_lo, core), fft: 16 (over x, z_hi).
Axes of the slice: x: 4, y: 4, z: 8 (z_hi: 4, z_lo: 2; z = z_hi * 2 + z_lo), core: 2. Of those that a mesh axis runs over, the one named last changes fastest.
Arguments:
- valence_store: bfloat16 [16, 64, 64, 64, 128], P('band', None, 'fft'), may hold values from -6 to 6
- valence_energy: float32 [64], replicated, may hold values from -12 to -1
- conduction: bfloat16 [16, 64, 64, 128], P('band', 'fft'), may hold values from -6 to 6
- conduction_energy: float32 [16], P('band'), may hold values from 1 to 40
- sphere_map: int32 [20480], replicated, may hold values from 0 to 262143, as said below
- owner: int32 [1], replicated, may hold values from 0 to 1023
Outputs:
- chi_window: float32 [2, 256, 20480], P(None, 'band', 'fft')
The draws below stay inside these ranges and needn't reach their ends.
Inputs may be any that keep to these rules, and one draw needn't show every extreme that they name: `sphere_map`: distinct flat cell indices x * 64 * 64 + y * 64 + z; they are the 20480 cells nearest the anchor, coordinates of 32 and above counting as negative frequencies, equally distant cells chosen from the seed, listed in an order drawn from the seed.
All inputs are finite; a program needn't handle non-finite values.
Results may differ from the reference program's by a relative error of at most 0.011.
Values may be sent and summed in bfloat16 or wider, within the bound.
No kernel may reach another device: no remote copies, remote signals or barrier semaphores. Data moves between devices by JAX's collectives and lax.ppermute only.
A program may use at most 320 MiB of HBM per device.

```python
import math
import jax
import jax.numpy as jnp
from jax import lax

NG = 64
NPW = 20480
NV = 64
NC = 16
COLS = 256
N_BAND = 16


def signed_frequency(coord):
    return jnp.where(coord < NG // 2, coord, coord - NG)


def draw_sphere_map(key, part):
    key = jax.random.fold_in(key, 7)
    order_key, shuffle_key = jax.random.split(key)
    cell_count = NG * NG * NG
    flat_index = jnp.arange(cell_count, dtype=jnp.int32)
    freq_x = signed_frequency(flat_index // (NG * NG))
    freq_y = signed_frequency(flat_index // NG % NG)
    freq_z = signed_frequency(flat_index % NG)
    radius_sq = freq_x * freq_x + freq_y * freq_y + freq_z * freq_z
    tiebreak = jax.random.permutation(order_key, cell_count).astype(jnp.int32)
    score = radius_sq * cell_count + tiebreak
    nearest = lax.top_k(-score, NPW)[1].astype(jnp.int32)
    shuffled = jax.random.permutation(shuffle_key, nearest)
    return shuffled.astype(jnp.int32)


def steps_of(rng, extent, cuts, smallest, largest):
    level, own = 1.0, jax.random.fold_in(rng, 6)
    for position, shards_of in cuts:
        steps = jnp.exp(jax.random.uniform(jax.random.fold_in(own, position), (shards_of,), jnp.float32, smallest / len(cuts), largest / len(cuts)))
        level = level * jnp.repeat(steps, extent[position] // shards_of).reshape([-1 if axis == position else 1 for axis in range(len(extent))])
    return level


def noise(rng, shape, scale, reach, shards=(), kind=jnp.bfloat16):
    drawn = scale * jax.random.normal(rng, shape, jnp.float32)
    if shards:
        drawn = drawn * steps_of(rng, shape, shards, -0.22, 0.18)
    return jnp.clip(drawn, -reach, reach).astype(kind)


def setup_inputs(seed: int = 0) -> dict:
    seeds = jax.random.split(jax.random.key(seed), 7)
    return {
        "valence_store": noise(seeds[0], (N_BAND, NV, NG, NG, 2 * NG), 1.0, 6.0, ((0, 16), (2, 16))),
        "valence_energy": jnp.clip(jax.random.uniform(seeds[1], (NV,), jnp.float32, -12.0, -1.0), -12.0, -1.0),
        "conduction": noise(seeds[2], (NC, NG, NG, 2 * NG), 1.0, 6.0, ((0, 16), (1, 16))),
        "conduction_energy": jnp.clip(1.0 + 39.0 * jax.random.uniform(seeds[3], (NC,), jnp.float32) ** steps_of(seeds[3], (NC,), ((0, 16),), -0.2, 0.2), 1.0, 40.0),
        "sphere_map": draw_sphere_map(jax.random.fold_in(seeds[6], 71), 0),
        "owner": jax.random.randint(seeds[5], (1,), 0, N_BAND * NV).astype(jnp.int32),
    }


def dft_table(length):
    steps_n = lax.broadcasted_iota(jnp.int32, (length, length), 0)
    steps_k = lax.broadcasted_iota(jnp.int32, (length, length), 1)
    phase_angle = 2.0 * math.pi / length * (steps_n * steps_k % length).astype(jnp.float32)
    factor = 1.0 / math.sqrt(length)
    cosine = jnp.cos(phase_angle) * factor
    sine_part = jnp.sin(phase_angle) * factor
    upper_half = jnp.stack([cosine, -sine_part], axis=1)
    lower_half = jnp.stack([sine_part, cosine], axis=1)
    return jnp.stack([upper_half, lower_half], axis=0).astype(jnp.bfloat16)

def pair_products(valence, conduction):
    length = valence.shape[-1] // 2
    val_re = valence[..., :length].astype(jnp.float32)[:, None]
    val_im = valence[..., length:].astype(jnp.float32)[:, None]
    con_re = conduction[..., :length].astype(jnp.float32)[None]
    con_im = conduction[..., length:].astype(jnp.float32)[None]
    real_part = val_re * con_re + val_im * con_im
    imag_part = val_re * con_im - val_im * con_re
    joined = jnp.concatenate([real_part, imag_part], axis=-1).astype(jnp.bfloat16)
    return joined.reshape((-1,) + joined.shape[2:])

def along_z(values_in, twiddle):
    length = twiddle.shape[1]
    square = twiddle.reshape(2 * length, 2 * length).astype(jnp.float32)
    mixed = jnp.einsum('axyn,nk->axyk', values_in.astype(jnp.float32), square)
    return mixed.astype(jnp.bfloat16)

def along_y(values_in, twiddle):
    length = twiddle.shape[1]
    split = values_in.reshape(values_in.shape[:3] + (2, length)).astype(jnp.float32)
    mixed = jnp.einsum('axypz,pyqk->axkqz', split, twiddle.astype(jnp.float32))
    return mixed.reshape(values_in.shape).astype(jnp.bfloat16)

def along_x(values_in, twiddle):
    length = twiddle.shape[1]
    split = values_in.reshape(values_in.shape[:3] + (2, length)).astype(jnp.float32)
    mixed = jnp.einsum('axypz,pxqk->aqkyz', split, twiddle.astype(jnp.float32))
    return mixed.astype(jnp.bfloat16)

def window_matrix(window, weights):
    scaled_re = (weights[:, None] * window[:, 0, :].astype(jnp.float32)).T
    scaled_im = (weights[:, None] * window[:, 1, :].astype(jnp.float32)).T
    first_row = jnp.stack([scaled_re, scaled_im], axis=2)
    second_row = jnp.stack([-scaled_im, scaled_re], axis=2)
    joined = jnp.stack([first_row, second_row], axis=0).astype(jnp.bfloat16)
    return joined.reshape(2 * joined.shape[1], 2 * joined.shape[2])

def reference(valence_store, valence_energy, conduction, conduction_energy, sphere_map, owner):
    slot_index = (owner[0] % N_BAND).astype(jnp.int32)
    valence = lax.dynamic_index_in_dim(valence_store, slot_index, 0, keepdims=False)
    twiddle = dft_table(NG)
    norm_scale = 1.0 / math.sqrt(NV * NC)

    def one_band(total, band_index):
        single = lax.dynamic_slice_in_dim(conduction, band_index, 1, 0)
        pair_grid = pair_products(valence, single)
        spectrum = along_x(along_y(along_z(pair_grid, twiddle), twiddle), twiddle)
        flat_grid = spectrum.reshape(NV, 2, NG * NG * NG)
        sphere = jnp.take(flat_grid, sphere_map, axis=2)
        energy = lax.dynamic_index_in_dim(conduction_energy, band_index, 0, keepdims=False)
        weights = 4.0 * norm_scale / (valence_energy - energy)
        left_side = window_matrix(sphere[:, :, :COLS], weights)
        right_side = sphere.reshape(2 * NV, NPW)
        term = jnp.dot(left_side, right_side, preferred_element_type=jnp.float32)
        return (total + term.reshape(2, COLS, NPW), band_index)
    start = jnp.zeros((2, COLS, NPW), jnp.float32)
    total, ignored = lax.scan(one_band, start, jnp.arange(NC, dtype=jnp.int32))
    return total
```

```python
import math

import jax
import jax.numpy as jnp
import numpy as np
from jax import lax
from jax.experimental import pallas as pl
from jax.experimental.pallas import tpu as pltpu
from jax.sharding import PartitionSpec as P

COL_DEV = 16
f32 = jnp.float32
bf16 = jnp.bfloat16

LENGTH = 64
RADIUS_SQ = 290
QUADS = sorted(
    (a * a + b * b, a, b) for a in range(18) for b in range(18) if a * a + b * b <= RADIUS_SQ
)
GROUPS = 4
SLOTS = 64
USED = -(-len(QUADS) // GROUPS)
HEIGHT = [int(math.isqrt(RADIUS_SQ - QUADS[GROUPS * s][0])) for s in range(USED)]
BASE = [sum(2 * (h + 1) for h in HEIGHT[:s]) for s in range(USED)]
CELLS = 1536
CAP = 128
assert BASE[-1] + 2 * (HEIGHT[-1] + 1) <= CELLS


def unit_table(rows, columns):
    angle = 2.0 * np.pi / LENGTH * (np.outer(rows, columns) % LENGTH)
    cosine = (np.cos(angle) / 8.0).astype(np.float32).astype(jnp.bfloat16)
    sine = (np.sin(angle) / 8.0).astype(np.float32).astype(jnp.bfloat16)
    return cosine.astype(np.float32), sine.astype(np.float32)


def plane_table():
    cosine, sine = unit_table(np.arange(18), np.arange(LENGTH))
    table = np.zeros((GROUPS, 4, SLOTS, LENGTH, LENGTH), np.float32)
    for index, (_, a, b) in enumerate(QUADS):
        g, s = index % GROUPS, index // GROUPS
        table[g, 0, s] = np.outer(cosine[a], cosine[b])
        table[g, 1, s] = np.outer(cosine[a], sine[b])
        table[g, 2, s] = np.outer(sine[a], cosine[b])
        table[g, 3, s] = np.outer(sine[a], sine[b])
    return table.reshape(GROUPS * 4 * SLOTS, LENGTH * LENGTH).astype(jnp.bfloat16)


def line_tables():
    cosine, sine = unit_table(np.arange(24), np.arange(LENGTH))
    return [
        np.concatenate([cosine[:n], sine[:n]], axis=0).astype(jnp.bfloat16) for n in (8, 16, 24)
    ]


def lookup_table():
    table = np.zeros((4, 18, 18), np.float32)
    for index, (_, a, b) in enumerate(QUADS):
        s = index // GROUPS
        table[:, a, b] = (index, BASE[s] // 16, BASE[s] % 16, HEIGHT[s] + 1)
    return table


def swap(value):
    lane = lax.broadcasted_iota(jnp.int32, value.shape, 1)
    turned = pltpu.roll(value, 64, 1)
    return jnp.where(lane < 64, turned, -turned)


def plane_kernel(
    val_ref, con_ref, table_ref, pick_ref, turn_ref, send_ref, part_ref, pair_ref, got_ref
):
    step = pl.program_id(0)

    @pl.when(step == 0)
    def _():
        got_ref[...] = jnp.zeros_like(got_ref)
        chunk = 512

        @pl.loop(0, LENGTH * LENGTH // chunk)
        def _(k):
            lanes = pl.ds(pl.multiple_of(k * chunk, chunk), chunk)
            for x in range(4):
                con_re = con_ref[2 * x, :, lanes].astype(f32)
                con_im = con_ref[2 * x + 1, :, lanes].astype(f32)
                for v in range(4):
                    val_re = val_ref[2 * x, pl.ds(v, 1), lanes]
                    val_im = val_ref[2 * x + 1, pl.ds(v, 1), lanes]
                    real = val_re * con_re + val_im * con_im
                    imag = val_re * con_im - val_im * con_re
                    pair_ref[pl.ds(x * 128 + v * 16, 16), lanes] = real.astype(bf16)
                    pair_ref[pl.ds(x * 128 + 64 + v * 16, 16), lanes] = imag.astype(bf16)

    mixed = lax.dot_general(
        table_ref[...], pair_ref[...], (((1,), (1,)), ((), ())), preferred_element_type=f32
    )
    for x in range(4):
        part = mixed[:, x * 128 : (x + 1) * 128]
        cc, cs, sc, ss = (part[SLOTS * i : SLOTS * (i + 1)] for i in range(4))
        sc, cs = swap(sc), swap(cs)
        same, other = cc - ss, cc + ss
        total, apart = sc + cs, sc - cs
        for variant, value in enumerate((same + total, other + apart, other - apart, same - total)):
            send_ref[variant, 0, x] = value.astype(bf16)
        columns = jnp.concatenate([send_ref[i, 0, x] for i in range(4)], axis=0)
        got_ref[:, x * 128 : (x + 1) * 128] += jnp.dot(
            pick_ref[...], columns, preferred_element_type=f32
        )

    @pl.when(step == GROUPS - 1)
    def _():
        total = jnp.zeros(part_ref.shape, f32)
        for x in range(4):
            value = got_ref[:, x * 128 : (x + 1) * 128]
            total += turn_ref[:, x : x + 1] * value
            total += swap(turn_ref[:, 4 + x : 5 + x] * value)
        part_ref[...] = total


def plane_call(val, con, table, pick, turn):
    return pl.pallas_call(
        plane_kernel,
        grid=(GROUPS,),
        in_specs=[
            pl.BlockSpec((8, 4, 4096), lambda g: (0, 0, 0)),
            pl.BlockSpec((8, 16, 4096), lambda g: (0, 0, 0)),
            pl.BlockSpec((4 * SLOTS, 4096), lambda g: (g, 0)),
            pl.BlockSpec((256, 4 * SLOTS), lambda g: (0, g)),
            pl.BlockSpec((256, 8), lambda g: (0, 0)),
        ],
        out_specs=[
            pl.BlockSpec((4, 1, 4, SLOTS, 128), lambda g: (0, g, 0, 0, 0)),
            pl.BlockSpec((256, 128), lambda g: (0, 0)),
        ],
        out_shape=[
            jax.ShapeDtypeStruct((4, GROUPS, 4, SLOTS, 128), bf16),
            jax.ShapeDtypeStruct((256, 128), f32),
        ],
        scratch_shapes=[pltpu.VMEM((512, 4096), bf16), pltpu.VMEM((256, 512), f32)],
        compiler_params=pltpu.CompilerParams(vmem_limit_bytes=48 * 1024 * 1024),
        cost_estimate=pl.CostEstimate(
            flops=2 * 1024 * 512 * 4096, bytes_accessed=12 << 20, transcendentals=0
        ),
    )(val, con, table, pick, turn)


def line_kernel(
    me_ref,
    grid_ref,
    line8_ref,
    line16_ref,
    line24_ref,
    window_ref,
    weight_ref,
    out_ref,
    wide_ref,
    rho_ref,
    left_ref,
):
    me = me_ref[0]
    lines = {8: line8_ref, 16: line16_ref, 24: line24_ref}

    @pl.loop(0, LENGTH)
    def _(x):
        wide_ref[pl.ds(pl.multiple_of(x * SLOTS, SLOTS), SLOTS), :] = grid_ref[x].astype(f32)

    last = BASE[-1] + 2 * (HEIGHT[-1] + 1)
    rho_ref[last - last % 8 :, :] = jnp.zeros((CELLS - last + last % 8, 128), f32)
    for first in range(0, USED, 2):
        both = jnp.concatenate(
            [wide_ref[pl.ds(first + i, LENGTH, stride=SLOTS), :] for i in range(2)], axis=1
        ).astype(bf16)
        rows = -(-(HEIGHT[first] + 1) // 8) * 8
        mixed = jnp.dot(lines[rows][...], both, preferred_element_type=f32)
        for i in range(2):
            count, base = HEIGHT[first + i] + 1, BASE[first + i]
            cosine = mixed[:rows, i * 128 : (i + 1) * 128]
            sine = swap(mixed[rows:, i * 128 : (i + 1) * 128])
            rho_ref[base : base + count, :] = (cosine + sine)[:count]
            rho_ref[base + count : base + 2 * count, :] = (cosine - sine)[:count]
    for b in range(COL_DEV):
        scaled = (weight_ref[...] * window_ref[b ^ me].astype(f32)).astype(bf16)
        left_ref[b * 32 : b * 32 + 16, :] = scaled
        left_ref[b * 32 + 16 : b * 32 + 32, :] = (-swap(scaled.astype(f32))).astype(bf16)
    for n in range(0, CELLS, 256):
        product = lax.dot_general(
            left_ref[...],
            rho_ref[n : n + 256, :].astype(bf16),
            (((1,), (1,)), ((), ())),
            preferred_element_type=f32,
        )
        out_ref[:, n : n + 256] = product.astype(bf16)


def line_call(me, grid, lines, window, weight):
    whole = pl.BlockSpec(memory_space=pltpu.VMEM)
    return pl.pallas_call(
        line_kernel,
        in_specs=[pl.BlockSpec(memory_space=pltpu.SMEM)] + [whole] * 6,
        out_shape=jax.ShapeDtypeStruct((512, CELLS), bf16),
        scratch_shapes=[
            pltpu.VMEM((LENGTH * SLOTS, 128), f32),
            pltpu.VMEM((CELLS, 128), f32),
            pltpu.VMEM((512, 128), bf16),
        ],
        compiler_params=pltpu.CompilerParams(vmem_limit_bytes=32 * 1024 * 1024),
        cost_estimate=pl.CostEstimate(
            flops=2 * 512 * 128 * CELLS, bytes_accessed=3 << 20, transcendentals=0
        ),
    )(me.reshape(1), grid, *lines, window, weight)


def split(value):
    high = value.astype(bf16)
    return high, (value - high.astype(f32)).astype(bf16)


def pick_kernel(parts_ref, rows_ref, out_ref, both_ref):
    for n in range(0, CELLS, 512):
        total = parts_ref[0, :, n : n + 512].astype(f32)
        for i in range(1, COL_DEV):
            total += parts_ref[i, :, n : n + 512].astype(f32)
        both_ref[:32, n : n + 512], both_ref[32:, n : n + 512] = split(total)
    for n in range(0, 16 * CAP, 256):
        cell = lax.broadcasted_iota(jnp.int32, (CELLS, 256), 0)
        chosen = jnp.where(cell == rows_ref[:, n : n + 256], 1.0, 0.0).astype(bf16)
        found = jnp.dot(both_ref[...], chosen, preferred_element_type=f32)
        found = found[:32] + found[32:]
        for i in range(256 // CAP):
            out_ref[n // CAP + i] = found[:, i * CAP : (i + 1) * CAP]


def pick_call(parts, rows):
    return pl.pallas_call(
        pick_kernel,
        out_shape=jax.ShapeDtypeStruct((16, 32, CAP), f32),
        scratch_shapes=[pltpu.VMEM((64, CELLS), bf16)],
        compiler_params=pltpu.CompilerParams(vmem_limit_bytes=32 * 1024 * 1024),
        cost_estimate=pl.CostEstimate(
            flops=2 * 64 * CELLS * 16 * CAP, bytes_accessed=2 << 20, transcendentals=0
        ),
    )(parts, rows)


def place_kernel(found_ref, place_ref, out_ref, both_ref):
    for i in range(16):
        both_ref[:32, i * CAP : (i + 1) * CAP], both_ref[32:, i * CAP : (i + 1) * CAP] = split(
            found_ref[i]
        )
    for n in range(0, out_ref.shape[1], 256):
        slot = lax.broadcasted_iota(jnp.int32, (16 * CAP, 256), 0)
        chosen = jnp.where(slot == place_ref[:, n : n + 256], 1.0, 0.0).astype(bf16)
        value = jnp.dot(both_ref[...], chosen, preferred_element_type=f32)
        out_ref[:, n : n + 256] = value[:32] + value[32:]


def place_call(found, place):
    return pl.pallas_call(
        place_kernel,
        out_shape=jax.ShapeDtypeStruct((32, place.shape[1]), f32),
        scratch_shapes=[pltpu.VMEM((64, 16 * CAP), bf16)],
        compiler_params=pltpu.CompilerParams(vmem_limit_bytes=32 * 1024 * 1024),
        cost_estimate=pl.CostEstimate(
            flops=2 * 64 * 16 * CAP * 1280, bytes_accessed=1 << 20, transcendentals=0
        ),
    )(found, place)


def route(sphere_map):
    def signed(coord):
        return jnp.where(coord < 32, coord, coord - 64)

    kx = signed(sphere_map // 4096)
    ky = signed(sphere_map // 64 % 64)
    kz = signed(sphere_map % 64)
    inside = jnp.all(kx * kx + ky * ky + kz * kz <= RADIUS_SQ)
    step = lax.broadcasted_iota(jnp.int32, (18, sphere_map.shape[0]), 0)
    hot_y = (step == jnp.abs(ky)[None]).astype(bf16)
    hot_z = (step == jnp.abs(kz)[None]).astype(f32)
    table = jnp.asarray(lookup_table().transpose(0, 2, 1).reshape(4 * 18, 18), bf16)
    found = jnp.dot(table, hot_y, preferred_element_type=f32).reshape(4, 18, -1)
    found = jnp.sum(found * hot_z[None], axis=1).astype(jnp.int32)
    quad, base, count = found[0], found[1] * 16 + found[2], found[3]
    variant = 2 * (ky < 0) + 1 * (kz < 0)
    group, slot = quad % GROUPS, quad // GROUPS
    device = variant * GROUPS + group
    column = group * 4 * SLOTS + variant * SLOTS + slot
    row = base + jnp.where(kx >= 0, kx, count - kx)
    return inside, device, column, row, kx


def spread(value, axis):
    copies = jnp.broadcast_to(value[None], (lax.axis_size(axis),) + value.shape)
    return lax.all_to_all(copies, axis, 0, 0, tiled=True)


def sum_and_spread(part, me):
    def far(value, step):
        return lax.ppermute(value, "fft", [(i, i ^ step) for i in range(16)])

    def block(value, index):
        return lax.dynamic_index_in_dim(value, index, 0, keepdims=False)

    part = part.reshape(4, 4, 16, 128)
    x, z = me // 4, me % 4
    total = block(part, x)
    for i in range(1, 4):
        total += far(block(part, x ^ i), 4 * i)
    value = block(total, z)
    for i in range(1, 4):
        value += far(block(total, z ^ i), i)
    value = value.astype(bf16)
    row = jnp.stack([value] + [far(value, i) for i in range(1, 4)])
    return jnp.concatenate([row] + [far(row, 4 * i) for i in range(1, 4)])


def on_device(valence_store, valence_energy, conduction, conduction_energy, sphere_map, owner):
    band_count, fft_count = lax.axis_size("band"), lax.axis_size("fft")
    me_band, me_fft = lax.axis_index("band"), lax.axis_index("fft")
    valence_total = valence_store.shape[1]
    conduction_total = conduction.shape[0] * band_count
    window_total = COL_DEV * band_count
    share = valence_total // band_count
    waves = sphere_map.shape[0] // fft_count

    slot_index = owner[0] % band_count
    blocks = valence_store.reshape((band_count, share) + valence_store.shape[2:])
    blocks = lax.all_to_all(blocks, "band", 0, 0, tiled=True)
    valence = lax.dynamic_index_in_dim(blocks, slot_index, 0, keepdims=False)
    val = valence.reshape(share, 4, 64, 2, 64).transpose(1, 3, 0, 2, 4).reshape(8, share, 4096)
    con = conduction.reshape(4, 64, 2, 64).transpose(0, 2, 1, 3).reshape(8, 4096)
    con = spread(con, "band").transpose(1, 0, 2)
    energies = spread(jnp.broadcast_to(conduction_energy, (1, 128)), "band")[:, 0, 0]

    inside, device, column, row, kx = route(sphere_map)
    by_block = device.reshape(fft_count, waves)
    devices = jnp.arange(fft_count, dtype=jnp.int32)
    counts = jnp.sum(
        (by_block[:, None, :] == devices[None, :, None]).astype(jnp.int32), axis=2
    )
    fits = inside & jnp.all(counts <= CAP)
    mine = by_block == me_fft
    own_block = lax.dynamic_index_in_dim(by_block, me_fft, 0, keepdims=False)
    from_device = own_block[None] == devices[:, None]
    masks = jnp.concatenate([mine, from_device], axis=0).astype(bf16)
    before = lax.broadcasted_iota(jnp.int32, (waves, waves), 0)
    upto = lax.broadcasted_iota(jnp.int32, (waves, waves), 1)
    order = jnp.dot(masks, (before <= upto).astype(bf16), preferred_element_type=f32)
    order = order.astype(jnp.int32) - 1
    slots = jnp.arange(CAP, dtype=jnp.int32)
    chosen = (mine & True)[:, :, None] & (order[:fft_count, :, None] == slots)
    row_block = row.reshape(fft_count, waves)
    halves = jnp.stack([row_block // 64, row_block % 64], axis=1).astype(bf16)
    listed = jnp.einsum(
        "fpg,fgs->fps", halves, chosen.astype(bf16), preferred_element_type=f32
    ).astype(jnp.int32)
    rows = (listed[:, 0] * 64 + listed[:, 1]).reshape(1, fft_count * CAP)
    rank = jnp.sum(jnp.where(from_device, order[fft_count:], 0), axis=0)
    place = (own_block * CAP + rank).reshape(1, waves)
    pick = (column[:window_total, None] == jnp.arange(4 * GROUPS * SLOTS)[None]).astype(bf16)
    x_here = 4 * me_fft + jnp.arange(4, dtype=jnp.int32)
    angle = 2.0 * math.pi / 64 * ((kx[:window_total, None] * x_here[None]) % 64).astype(f32)
    turn = jnp.concatenate([jnp.cos(angle) / 8.0, jnp.sin(angle) / 8.0], axis=1)
    turn = turn.astype(bf16).astype(f32)

    planes, part = plane_call(val.astype(f32), con, jnp.asarray(plane_table()), pick, turn)
    grid = lax.all_to_all(planes.reshape(16, 4, SLOTS, 128), "fft", 0, 0, tiled=True)

    window = sum_and_spread(part, me_fft)
    norm_scale = 1.0 / math.sqrt(valence_total * conduction_total)
    own_energy = lax.dynamic_slice_in_dim(valence_energy, me_band * share, share, 0)
    weight = (4.0 * norm_scale / (own_energy[:, None] - energies[None, :])).reshape(1, -1)
    weight = jnp.concatenate([weight, weight], axis=1)

    lines = [jnp.asarray(table) for table in line_tables()]
    partial = line_call(me_fft, grid.reshape(64, SLOTS, 128), lines, window, weight)
    parts = lax.all_to_all(partial.reshape(band_count, 32, CELLS), "band", 0, 0, tiled=True)
    found = pick_call(parts, rows)
    found = lax.all_to_all(found, "fft", 0, 0, tiled=True)
    result = place_call(found, place).reshape(2, COL_DEV, waves)
    args = (valence_store, valence_energy, conduction, conduction_energy, sphere_map, owner)
    return lax.cond(fits, lambda *_: result, general_path, *args)


def broadcast(value, axis, source):
    kept = jnp.where(lax.axis_index(axis) == source, value, 0).astype(value.dtype)
    return lax.psum(kept, axis)


def dft_table(length):
    steps_n = lax.broadcasted_iota(jnp.int32, (length, length), 0)
    steps_k = lax.broadcasted_iota(jnp.int32, (length, length), 1)
    phase_angle = 2.0 * math.pi / length * (steps_n * steps_k % length).astype(jnp.float32)
    factor = 1.0 / math.sqrt(length)
    cosine = jnp.cos(phase_angle) * factor
    sine_part = jnp.sin(phase_angle) * factor
    upper_half = jnp.stack([cosine, -sine_part], axis=1)
    lower_half = jnp.stack([sine_part, cosine], axis=1)
    return jnp.stack([upper_half, lower_half], axis=0).astype(jnp.bfloat16)


def pair_products(valence, conduction):
    length = valence.shape[-1] // 2
    val_re = valence[..., :length].astype(jnp.float32)[:, None]
    val_im = valence[..., length:].astype(jnp.float32)[:, None]
    con_re = conduction[..., :length].astype(jnp.float32)[None]
    con_im = conduction[..., length:].astype(jnp.float32)[None]
    real_part = val_re * con_re + val_im * con_im
    imag_part = val_re * con_im - val_im * con_re
    joined = jnp.concatenate([real_part, imag_part], axis=-1).astype(jnp.bfloat16)
    return joined.reshape((-1,) + joined.shape[2:])


def along_z(values_in, twiddle):
    length = twiddle.shape[1]
    square = twiddle.reshape(2 * length, 2 * length)
    return jnp.dot(values_in, square, preferred_element_type=jnp.float32).astype(jnp.bfloat16)


def along_y(values_in, twiddle):
    length = twiddle.shape[1]
    split = values_in.reshape(values_in.shape[:3] + (2, length))
    mixed = jnp.einsum("axypz,pyqk->axkqz", split, twiddle, preferred_element_type=jnp.float32)
    return mixed.reshape(values_in.shape).astype(jnp.bfloat16)


def along_x(values_in, twiddle):
    length = twiddle.shape[1]
    split = values_in.reshape(values_in.shape[:3] + (2, length))
    mixed = jnp.einsum("axypz,pxqk->aqkyz", split, twiddle, preferred_element_type=jnp.float32)
    return mixed.astype(jnp.bfloat16)


def window_matrix(window, weights):
    scaled_re = (weights[:, None] * window[:, 0, :].astype(jnp.float32)).T
    scaled_im = (weights[:, None] * window[:, 1, :].astype(jnp.float32)).T
    first_row = jnp.stack([scaled_re, scaled_im], axis=2)
    second_row = jnp.stack([-scaled_im, scaled_re], axis=2)
    joined = jnp.stack([first_row, second_row], axis=0).astype(jnp.bfloat16)
    return joined.reshape(2 * joined.shape[1], 2 * joined.shape[2])


def general_path(valence_store, valence_energy, conduction, conduction_energy, sphere_map, owner):
    band_count = lax.axis_size("band")
    conduction_dev = conduction.shape[0]
    valence_total = valence_store.shape[1]
    length = conduction.shape[2]
    norm_scale = 1.0 / math.sqrt(valence_total * conduction_dev * band_count)
    twiddle = dft_table(length)
    window_total = COL_DEV * band_count
    slot_index = owner[0] % band_count
    valence = broadcast(valence_store, "band", slot_index)[0]
    pair_grid = along_y(along_z(pair_products(valence, conduction), twiddle), twiddle)
    weights = (4.0 * norm_scale / (valence_energy[:, None] - conduction_energy[None, :])).reshape(
        -1
    )
    whole_grids = lax.all_to_all(pair_grid, "fft", split_axis=0, concat_axis=1, tiled=True)
    spectrum = along_x(whole_grids, twiddle)
    flat_grid = spectrum.reshape(spectrum.shape[0], 2, -1)
    sphere = jnp.take(flat_grid, sphere_map, axis=2)
    row_block = lax.all_to_all(sphere, "fft", split_axis=2, concat_axis=0, tiled=True)
    window = lax.all_gather(sphere[:, :, :window_total], "fft", axis=0, tiled=True)
    left_side = window_matrix(window, weights)
    right_side = row_block.reshape(-1, row_block.shape[2])
    product = jnp.dot(left_side, right_side, preferred_element_type=jnp.float32)
    partial_value = product.reshape(2, window_total, -1)
    return lax.psum_scatter(partial_value, "band", scatter_dimension=1, tiled=True)


def solution(mesh):
    placed = (
        P("band", None, "fft", None, None),
        P(),
        P("band", "fft", None, None),
        P("band"),
        P(),
        P(),
    )
    return jax.shard_map(
        on_device, mesh=mesh, in_specs=placed, out_specs=P(None, "band", "fft"), check_vma=False
    )
```

```python
import functools
import math

import jax
import jax.numpy as jnp
import numpy as np
from jax import lax
from jax.experimental import pallas as pl
from jax.experimental.pallas import tpu as pltpu
from jax.sharding import Mesh
from jax.sharding import PartitionSpec as P

COL_DEV = 16
f32 = jnp.float32
bf16 = jnp.bfloat16

LENGTH = 64
RADIUS_SQ = 290
QUADS = sorted(
    (a * a + b * b, a, b)
    for a in range(18)
    for b in range(18)
    if a * a + b * b <= RADIUS_SQ and (a > 0 or b == 0)
)
GROUPS = 16
SLOTS = 16
USED = -(-len(QUADS) // GROUPS)
HEIGHT = [int(math.isqrt(RADIUS_SQ - QUADS[GROUPS * s][0])) for s in range(USED)]
BASE = [sum(2 * h + 1 for h in HEIGHT[:s]) for s in range(USED)]
ROWS = 384
CELLS = 4 * ROWS
CAP = 128
assert USED < SLOTS and BASE[-1] + 2 * HEIGHT[-1] + 1 <= ROWS

AXES = {"y": 4, "zl": 2, "c": 2, "x": 4, "zh": 4}
BAND = ("y", "zl", "c")
FFT = ("x", "zh")
NEAR = ("zl", "c", "x", "zh")


def unit_table(rows, columns):
    angle = 2.0 * np.pi / LENGTH * (np.outer(rows, columns) % LENGTH)
    cosine = (np.cos(angle) / 8.0).astype(np.float32).astype(jnp.bfloat16)
    sine = (np.sin(angle) / 8.0).astype(np.float32).astype(jnp.bfloat16)
    return cosine.astype(np.float32), sine.astype(np.float32)


def plane_table():
    cosine, sine = unit_table(np.arange(18), np.arange(LENGTH))
    table = np.zeros((4, 4, 4, SLOTS, LENGTH, LENGTH), np.float32)
    for index, (_, a, b) in enumerate(QUADS):
        g, s = index % GROUPS, index // GROUPS
        if b == 0 and a > 0:
            first, second = np.outer(cosine[a], cosine[0]), np.outer(cosine[0], cosine[a])
            turned, across = np.outer(sine[a], cosine[0]), np.outer(cosine[0], sine[a])
            kinds = (first + second, turned - across, turned + across, second - first)
            kinds = [0.5 * kind for kind in kinds]
        else:
            kinds = (
                np.outer(cosine[a], cosine[b]),
                np.outer(cosine[a], sine[b]),
                np.outer(sine[a], cosine[b]),
                np.outer(sine[a], sine[b]),
            )
        for kind in range(4):
            table[g // 4, kind, g % 4, s] = kinds[kind]
    return table.reshape(GROUPS * 4 * SLOTS, LENGTH * LENGTH).astype(jnp.bfloat16)


def line_tables():
    cosine, sine = unit_table(np.arange(24), np.arange(LENGTH))
    return [
        np.concatenate([cosine[:n], sine[:n]], axis=0).astype(jnp.bfloat16) for n in (8, 16, 24)
    ]


def lookup_table():
    table = np.zeros((4, 18, 18), np.float32)
    for index, (_, a, b) in enumerate(QUADS):
        s = index // GROUPS
        table[:, a, b] = (index, BASE[s] // 16, BASE[s] % 16, HEIGHT[s])
        if b == 0:
            table[:, 0, a] = table[:, a, b]
    return table


def swap(value):
    lane = lax.broadcasted_iota(jnp.int32, value.shape, 1)
    turned = pltpu.roll(value, 64, 1)
    return jnp.where(lane < 64, turned, -turned)


def route_kernel(map_ref, table_ref, out_ref):
    out_ref[...] = jnp.zeros_like(out_ref)
    step = lax.broadcasted_iota(jnp.int32, (32, 2048), 0)
    for n in range(0, map_ref.shape[1], 2048):
        lanes = slice(n, n + 2048)
        cell = map_ref[:, lanes]
        coords = (cell >> 12, (cell >> 6) & 63, cell & 63)
        kx, ky, kz = (jnp.where(coord < 32, coord, coord - 64) for coord in coords)
        inside = kx * kx + ky * ky + kz * kz <= RADIUS_SQ
        hot_y = jnp.where(step == jnp.abs(ky), 1.0, 0.0).astype(bf16)
        hot_z = jnp.where(step == jnp.abs(kz), 1.0, 0.0)
        found = jnp.dot(table_ref[...], hot_y, preferred_element_type=f32)
        found = [
            jnp.sum(found[32 * i : 32 * i + 32] * hot_z, axis=0, keepdims=True).astype(jnp.int32)
            for i in range(4)
        ]
        quad, base, height = found[0], found[1] * 16 + found[2], found[3]
        group, slot = quad & (GROUPS - 1), quad >> 4
        variant = jnp.where(ky < 0, 2, 0) + jnp.where(kz < 0, 1, 0)
        variant = jnp.where(kz == 0, jnp.where(ky < 0, 3, 0), variant)
        variant = jnp.where((ky == 0) & (kz != 0), jnp.where(kz < 0, 2, 1), variant)
        out_ref[0:1, lanes] = group
        row = variant * ROWS + base + jnp.where(kx >= 0, kx, height - kx)
        out_ref[1:2, lanes] = row
        out_ref[2:3, lanes] = jnp.where(inside, 1, 0)


def window_kernel(cell_ref, unit_ref, out_ref):
    cell = cell_ref[...]
    step = lax.broadcasted_iota(jnp.int32, (256, 32), 1)
    lane = lax.broadcasted_iota(jnp.int32, (256, 128), 1)
    units = []
    for coord in ((cell >> 6) & 63, cell & 63):
        freq = jnp.where(coord < 32, coord, coord - 64)
        hot = jnp.where(step == jnp.abs(freq), 1.0, 0.0).astype(bf16)
        unit = jnp.dot(hot, unit_ref[...], preferred_element_type=f32)
        units.append(jnp.where((lane >= 64) & (freq < 0), -unit, unit))
    along_y, along_z = units
    turned = pltpu.roll(along_z, 64, 1)
    cos_z = jnp.where(lane < 64, along_z, turned)
    sin_z = jnp.where(lane < 64, turned, along_z)
    for y in range(0, LENGTH, 2):
        cos_y = jnp.where(lane < 64, along_y[:, y : y + 1], along_y[:, y + 1 : y + 2])
        sin_y = jnp.where(lane < 64, along_y[:, 64 + y : 65 + y], along_y[:, 65 + y : 66 + y])
        lanes = slice(y * 64, y * 64 + 128)
        out_ref[:256, lanes] = (cos_y * cos_z - sin_y * sin_z).astype(bf16)
        out_ref[256:, lanes] = (sin_y * cos_z + cos_y * sin_z).astype(bf16)


def window_call(cells):
    unit = np.concatenate(unit_table(np.arange(32), np.arange(LENGTH)), axis=1)
    return pl.pallas_call(
        window_kernel,
        out_shape=jax.ShapeDtypeStruct((512, 4096), bf16),
        compiler_params=pltpu.CompilerParams(vmem_limit_bytes=16 * 1024 * 1024),
        cost_estimate=pl.CostEstimate(
            flops=16 * 512 * 4096, bytes_accessed=4 << 20, transcendentals=0
        ),
    )(cells.reshape(256, 1), jnp.asarray(unit, bf16))


def route(sphere_map):
    waves = sphere_map.shape[0]
    table = np.zeros((4, 32, 32), np.float32)
    table[:, :18, :18] = lookup_table().transpose(0, 2, 1)
    return pl.pallas_call(
        route_kernel,
        out_shape=jax.ShapeDtypeStruct((8, waves), jnp.int32),
        compiler_params=pltpu.CompilerParams(vmem_limit_bytes=8 * 1024 * 1024),
        cost_estimate=pl.CostEstimate(
            flops=2 * 128 * 32 * waves, bytes_accessed=40 * waves, transcendentals=0
        ),
    )(sphere_map.reshape(1, waves), jnp.asarray(table.reshape(128, 32), bf16))


def pair_kernel(
    first_ref,
    second_ref,
    con_ref,
    table_ref,
    turn_ref,
    pair_ref,
    part_ref,
    wide_ref,
    val_ref,
    buffer_ref,
    sem_ref,
):
    copy = pltpu.make_async_copy(table_ref, buffer_ref, sem_ref)
    copy.start()
    for band in range(2):
        for x in range(4):
            start = (band * 4 + x) * 64
            wide_ref[start : start + 64, :] = first_ref[band, x].astype(f32)
            wide_ref[512 + start : 576 + start, :] = second_ref[band, x].astype(f32)
    left = lax.broadcasted_iota(jnp.int32, (4, 128), 1) < 64

    for y in range(0, LENGTH, 2):
        lanes = slice(y * 64, y * 64 + 128)
        for x in range(4):
            even = wide_ref[pl.ds(x * 64 + y, 4, stride=256), :]
            odd = wide_ref[pl.ds(x * 64 + y + 1, 4, stride=256), :]
            val_ref[2 * x, :, lanes] = jnp.where(left, even, pltpu.roll(odd, 64, 1))
            val_ref[2 * x + 1, :, lanes] = jnp.where(left, pltpu.roll(even, 64, 1), odd)

    chunk = 512

    @pl.loop(0, LENGTH * LENGTH // chunk)
    def _(k):
        lanes = pl.ds(pl.multiple_of(k * chunk, chunk), chunk)
        for x in range(4):
            con_re = con_ref[2 * x, :, lanes].astype(f32)
            con_im = con_ref[2 * x + 1, :, lanes].astype(f32)
            for v in range(4):
                val_re = val_ref[2 * x, pl.ds(v, 1), lanes]
                val_im = val_ref[2 * x + 1, pl.ds(v, 1), lanes]
                real = val_re * con_re + val_im * con_im
                imag = val_re * con_im - val_im * con_re
                pair_ref[pl.ds(x * 128 + v * 16, 16), lanes] = real.astype(bf16)
                pair_ref[pl.ds(x * 128 + 64 + v * 16, 16), lanes] = imag.astype(bf16)

    copy.wait()
    total = jnp.zeros(part_ref.shape, f32)
    for x in range(4):
        mixed = lax.dot_general(
            buffer_ref[...],
            pair_ref[x * 128 : (x + 1) * 128, :],
            (((1,), (1,)), ((), ())),
            preferred_element_type=f32,
        )
        value = mixed[:256] + swap(mixed[256:])
        total += turn_ref[:, x : x + 1] * value
        total += swap(turn_ref[:, 4 + x : 5 + x] * value)
    part_ref[...] = total


def pair_call(first, second, con, table, turn):
    whole = pl.BlockSpec(memory_space=pltpu.VMEM)
    table = pltpu.with_memory_space_constraint(table, pltpu.HBM)
    return pl.pallas_call(
        pair_kernel,
        in_specs=[whole] * 3 + [pl.BlockSpec(memory_space=pltpu.HBM), whole],
        out_shape=[
            pltpu.VMEM((512, 4096), bf16),
            jax.ShapeDtypeStruct((256, 128), f32),
        ],
        scratch_shapes=[
            pltpu.VMEM((1024, 128), f32),
            pltpu.VMEM((8, 4, 4096), f32),
            pltpu.VMEM((512, 4096), bf16),
            pltpu.SemaphoreType.DMA,
        ],
        compiler_params=pltpu.CompilerParams(vmem_limit_bytes=22 * 1024 * 1024),
        cost_estimate=pl.CostEstimate(
            flops=2 * 512 * 512 * 4096, bytes_accessed=10 << 20, transcendentals=0
        ),
    )(first, second, con, table, turn)


def plane_kernel(pair_ref, table_ref, send_ref, buffer_ref, sem_ref):
    copies = [
        pltpu.make_async_copy(
            table_ref.at[pl.ds(i * 256, 256)], buffer_ref.at[i], sem_ref.at[i]
        )
        for i in range(4)
    ]
    for copy in copies:
        copy.start()
    for i in range(4):
        copies[i].wait()
        mixed = lax.dot_general(
            buffer_ref[i], pair_ref[...], (((1,), (1,)), ((), ())), preferred_element_type=f32
        )
        for x in range(4):
            part = mixed[:, x * 128 : (x + 1) * 128]
            cc, cs, sc, ss = (part[64 * k : 64 * (k + 1)] for k in range(4))
            sc, cs = swap(sc), swap(cs)
            same, other = cc - ss, cc + ss
            total, apart = sc + cs, sc - cs
            signs = (same + total, other + apart, other - apart, same - total)
            columns = jnp.concatenate([value.astype(bf16) for value in signs], axis=0)
            send_ref[:, 4 * i : 4 * i + 4, x] = columns.reshape(4, 4, SLOTS, 128)


def plane_call(pairs, table):
    return pl.pallas_call(
        plane_kernel,
        in_specs=[
            pl.BlockSpec(memory_space=pltpu.VMEM),
            pl.BlockSpec(memory_space=pltpu.HBM),
        ],
        out_shape=jax.ShapeDtypeStruct((4, GROUPS, 4, SLOTS, 128), bf16),
        scratch_shapes=[pltpu.VMEM((4, 256, 4096), bf16), pltpu.SemaphoreType.DMA((4,))],
        compiler_params=pltpu.CompilerParams(vmem_limit_bytes=24 * 1024 * 1024),
        cost_estimate=pl.CostEstimate(
            flops=2 * 1024 * 512 * 4096, bytes_accessed=8 << 20, transcendentals=0
        ),
    )(pairs, pltpu.with_memory_space_constraint(table, pltpu.HBM))


def line_kernel(
    me_ref,
    grid_ref,
    line8_ref,
    line16_ref,
    line24_ref,
    window_ref,
    weight_ref,
    out_ref,
    wide_ref,
    rho_ref,
    left_ref,
):
    lines = {8: line8_ref, 16: line16_ref, 24: line24_ref}

    @pl.loop(0, 4 * LENGTH, step=4)
    def _(x):
        for i in range(4):
            start = pl.multiple_of((x + i) * SLOTS, SLOTS)
            wide_ref[pl.ds(start, SLOTS), :] = grid_ref[x + i].astype(f32)

    last = BASE[-1] + 2 * HEIGHT[-1] + 1
    rho_ref[last - last % 8 :, :] = jnp.zeros((ROWS - last + last % 8, 512), f32)
    for slot in range(USED):
        lane_tiles = [
            wide_ref[pl.ds(q * LENGTH * SLOTS + slot, LENGTH, stride=SLOTS), :] for q in range(4)
        ]
        values = jnp.concatenate(lane_tiles, axis=1).astype(bf16)
        count, base = HEIGHT[slot] + 1, BASE[slot]
        rows = -(-count // 8) * 8
        mixed = jnp.dot(lines[rows][...], values, preferred_element_type=f32)
        for q in range(4):
            lanes = slice(q * 128, (q + 1) * 128)
            cosine, sine = mixed[:rows, lanes], swap(mixed[rows:, lanes])
            rho_ref[base + count - 1 : base + 2 * count - 1, lanes] = (cosine - sine)[:count]
            rho_ref[base : base + count, lanes] = (cosine + sine)[:count]

    me = me_ref[0]
    wave = lax.broadcasted_iota(jnp.int32, (256, 1024), 0)
    column = lax.broadcasted_iota(jnp.int32, (256, 1024), 1)
    for q in range(4):
        lanes = slice(q * 128, (q + 1) * 128)
        place = ((q * 16 + wave // 16) ^ me) * 16 + wave % 16
        order = jnp.where(column == place, 1.0, 0.0).astype(bf16)
        values = jnp.dot(order, window_ref[...], preferred_element_type=f32)
        scaled = (weight_ref[:, lanes] * values).astype(bf16).astype(f32)
        turned = -swap(scaled)
        for b in range(COL_DEV):
            left_ref[b * 32 : b * 32 + 16, lanes] = scaled[b * 16 : b * 16 + 16].astype(bf16)
            left_ref[b * 32 + 16 : b * 32 + 32, lanes] = turned[b * 16 : b * 16 + 16].astype(bf16)
    for n in range(0, ROWS, 128):
        product = lax.dot_general(
            left_ref[...],
            rho_ref[n : n + 128, :].astype(bf16),
            (((1,), (1,)), ((), ())),
            preferred_element_type=f32,
        )
        out_ref[:, n : n + 128] = product.astype(bf16)


def line_call(me, grid, lines, window, weight):
    whole = pl.BlockSpec(memory_space=pltpu.VMEM)
    return pl.pallas_call(
        line_kernel,
        in_specs=[pl.BlockSpec(memory_space=pltpu.SMEM)] + [whole] * 6,
        out_shape=jax.ShapeDtypeStruct((512, ROWS), bf16),
        scratch_shapes=[
            pltpu.VMEM((4 * LENGTH * SLOTS, 128), f32),
            pltpu.VMEM((ROWS, 512), f32),
            pltpu.VMEM((512, 512), bf16),
        ],
        compiler_params=pltpu.CompilerParams(vmem_limit_bytes=16 * 1024 * 1024),
        cost_estimate=pl.CostEstimate(
            flops=2 * 512 * 512 * ROWS, bytes_accessed=3 << 20, transcendentals=0
        ),
    )(me.reshape(1), grid, *lines, window, weight)


def split(value):
    high = value.astype(bf16)
    return high, (value - high.astype(f32)).astype(bf16)


def pick_kernel(parts_ref, rows_ref, out_ref, both_ref):
    for q in range(4):
        lanes = slice(q * ROWS, (q + 1) * ROWS)
        total = parts_ref[q].astype(f32)
        for y in range(1, 4):
            total += parts_ref[4 * y + q].astype(f32)
        both_ref[:32, lanes], both_ref[32:, lanes] = split(total)
    for n in range(0, 16 * CAP, 256):
        cell = lax.broadcasted_iota(jnp.int32, (CELLS, 256), 0)
        chosen = jnp.where(cell == rows_ref[:, n : n + 256], 1.0, 0.0).astype(bf16)
        found = jnp.dot(both_ref[...], chosen, preferred_element_type=f32)
        found = found[:32] + found[32:]
        for i in range(256 // CAP):
            out_ref[n // CAP + i] = found[:, i * CAP : (i + 1) * CAP]


def pick_call(parts, rows):
    return pl.pallas_call(
        pick_kernel,
        out_shape=jax.ShapeDtypeStruct((16, 32, CAP), f32),
        scratch_shapes=[pltpu.VMEM((64, CELLS), bf16)],
        compiler_params=pltpu.CompilerParams(vmem_limit_bytes=16 * 1024 * 1024),
        cost_estimate=pl.CostEstimate(
            flops=2 * 64 * CELLS * 16 * CAP, bytes_accessed=2 << 20, transcendentals=0
        ),
    )(parts, rows)


def place_kernel(found_ref, place_ref, out_ref, both_ref):
    for i in range(16):
        both_ref[:32, i * CAP : (i + 1) * CAP], both_ref[32:, i * CAP : (i + 1) * CAP] = split(
            found_ref[i]
        )
    for n in range(0, out_ref.shape[1], 256):
        slot = lax.broadcasted_iota(jnp.int32, (16 * CAP, 256), 0)
        chosen = jnp.where(slot == place_ref[:, n : n + 256], 1.0, 0.0).astype(bf16)
        value = jnp.dot(both_ref[...], chosen, preferred_element_type=f32)
        out_ref[:, n : n + 256] = value[:32] + value[32:]


def place_call(found, place):
    return pl.pallas_call(
        place_kernel,
        out_shape=jax.ShapeDtypeStruct((32, place.shape[1]), f32),
        scratch_shapes=[pltpu.VMEM((64, 16 * CAP), bf16)],
        compiler_params=pltpu.CompilerParams(vmem_limit_bytes=16 * 1024 * 1024),
        cost_estimate=pl.CostEstimate(
            flops=2 * 64 * 16 * CAP * 1280, bytes_accessed=1 << 20, transcendentals=0
        ),
    )(found, place)


def block(value, index):
    return lax.dynamic_index_in_dim(value, index, 0, keepdims=False)


def far(value, axis, step):
    size = math.prod(AXES[name] for name in (axis if isinstance(axis, tuple) else (axis,)))
    return lax.ppermute(value, axis, [(i, i ^ step) for i in range(size)])


def scatter_inputs(store, con, slot_index, sphere_map):
    y, zl, c = (lax.axis_index(name) for name in BAND)
    from_y, from_zl, from_c = slot_index // 4, slot_index // 2 % 2, slot_index % 2
    sent, con = lax.optimization_barrier((block(store, 1 - c), con))
    other = far(sent, "c", 1)
    held = jnp.where(c == from_c, block(store, c), other)

    def along_rows(value):
        mine = block(value, y)
        for step in range(1, 4):
            mine = jnp.where(y ^ from_y == step, far(block(value, y ^ step), "y", step), mine)
        return mine

    def along_pairs(value):
        return jnp.where(zl == from_zl, block(value, zl), far(block(value, 1 - zl), "zl", 1))

    rows = jnp.stack([con] + [far(con, "y", step) for step in range(1, 4)])
    later = held[:, :, 2:].swapaxes(0, 1)
    rows, sphere_map, _ = lax.optimization_barrier((rows, sphere_map, block(later, 1 - zl)))
    pairs = jnp.stack([rows, far(rows, "zl", 1)], axis=1)
    both = jnp.stack([pairs, far(pairs, "c", 1)], axis=2)
    first = along_pairs(along_rows(held[:, :, :2]))
    second = along_rows(along_pairs(later))
    return first, second, both.reshape((16,) + con.shape), sphere_map


def window_and_planes(pairs, part, table):
    x = lax.axis_index("x")
    part = part.reshape(4, 4, 16, 128)
    got = [block(part, x)] + [far(block(part, x ^ step), "x", step) for step in range(1, 4)]
    planes = plane_call(pairs, table)
    got, planes = lax.optimization_barrier((got, planes))
    total = got[0] + got[1] + got[2] + got[3]
    got = [far(total, "zh", step) for step in range(1, 4)]
    got[0], planes = lax.optimization_barrier((got[0], planes))
    return (total + got[0] + got[1] + got[2]).astype(bf16), planes


def gather_window(value):
    value = jnp.stack([value] + [far(value, "x", step) for step in range(1, 4)])
    return jnp.stack([value] + [far(value, ("zl", "c"), step) for step in range(1, 4)])


def on_device(valence_store, valence_energy, conduction, conduction_energy, sphere_map, owner):
    band_count, fft_count = lax.axis_size(BAND), lax.axis_size(FFT)
    me_band, me_fft, me_near = (lax.axis_index(axis) for axis in (BAND, FFT, NEAR))
    valence_total = valence_store.shape[1]
    conduction_total = conduction.shape[0] * band_count
    window_total = COL_DEV * band_count
    share = valence_total // band_count
    waves = sphere_map.shape[0] // fft_count

    con = conduction.reshape(4, 64, 2, 64).transpose(0, 2, 1, 3).reshape(8, 4096)
    energy, pieces = conduction_energy[0], []
    for _ in range(3):
        pieces.append(lax.reduce_precision(energy, 8, 7))
        energy = energy - pieces[-1]
    extra = jnp.zeros((8, 128), f32).at[0, :3].set(jnp.stack(pieces)).astype(bf16)
    con = jnp.concatenate([con, extra], axis=1)
    store = valence_store.reshape((2, 4, 2, share) + valence_store.shape[2:])
    slot_index = owner[0] % band_count
    first, second, con, sphere_map = scatter_inputs(store, con, slot_index, sphere_map)
    energies = jnp.sum(con[:, 0, 4096:4099].astype(f32), axis=1)
    con = con[:, :, :4096].transpose(1, 0, 2)

    window_cells = sphere_map[:window_total]
    window_table = window_call(window_cells)
    kx = (window_cells // 4096)[:, None]
    x_here = 4 * me_fft + jnp.arange(4, dtype=jnp.int32)
    angle = 2.0 * math.pi / 64 * ((kx * x_here[None]) % 64).astype(f32)
    turn = jnp.concatenate([jnp.cos(angle) / 8.0, jnp.sin(angle) / 8.0], axis=1)
    turn = turn.astype(bf16).astype(f32)

    pairs, part = pair_call(first, second, con, window_table, turn)
    part, planes = window_and_planes(pairs, part, jnp.asarray(plane_table()))
    window = gather_window(part)
    sphere_map = lax.optimization_barrier((sphere_map, planes))[0]

    routed = route(sphere_map)
    by_block = routed[0].reshape(fft_count, waves)
    devices = jnp.arange(fft_count, dtype=jnp.int32)
    counts = jnp.sum(
        (by_block[:, None, :] == devices[None, :, None]).astype(jnp.int32), axis=2
    )
    fits = jnp.all(routed[2] == 1) & jnp.all(counts <= CAP)
    mine = by_block == me_fft
    own_block = lax.dynamic_index_in_dim(by_block, me_fft, 0, keepdims=False)
    from_device = own_block[None] == devices[:, None]
    masks = jnp.concatenate([mine, from_device], axis=0).astype(bf16)
    before = lax.broadcasted_iota(jnp.int32, (waves, waves), 0)
    upto = lax.broadcasted_iota(jnp.int32, (waves, waves), 1)
    order = jnp.dot(masks, (before <= upto).astype(bf16), preferred_element_type=f32)
    order = order.astype(jnp.int32) - 1
    slots = jnp.arange(CAP, dtype=jnp.int32)
    chosen = mine[:, :, None] & (order[:fft_count, :, None] == slots)
    row_block = routed[1].reshape(fft_count, waves)
    halves = jnp.stack([row_block // 64, row_block % 64], axis=1).astype(bf16)
    listed = jnp.einsum(
        "fpg,fgs->fps", halves, chosen.astype(bf16), preferred_element_type=f32
    ).astype(jnp.int32)
    rows = (listed[:, 0] * 64 + listed[:, 1]).reshape(1, fft_count * CAP)
    rank = jnp.sum(jnp.where(from_device, order[fft_count:], 0), axis=0)
    place = (own_block * CAP + rank).reshape(1, waves)
    grid = lax.all_to_all(planes.reshape(64, 4, SLOTS, 128), NEAR, 0, 0, tiled=True)
    norm_scale = 1.0 / math.sqrt(valence_total * conduction_total)
    near = jnp.arange(4, dtype=jnp.int32)
    bands = (near % 2) * 8 + lax.axis_index("y") * 2 + near // 2
    hot = bands[:, None, None] == (jnp.arange(valence_total) // share)[None, None, :]
    hot = hot & (jnp.arange(share)[None, :, None] == (jnp.arange(valence_total) % share))
    near_valence = jnp.sum(jnp.where(hot, valence_energy, 0.0), axis=2)
    steps = jnp.arange(band_count, dtype=jnp.int32)
    places = (near ^ (me_band % 4))[:, None] ^ steps[None, :]
    near_conduction = jnp.sum(
        jnp.where(places[:, :, None] == steps[None, None, :], energies, 0.0), axis=2
    )
    weight = 4.0 * norm_scale / (near_valence[:, :, None] - near_conduction[:, None, :])
    weight = jnp.broadcast_to(weight.reshape(4, 1, 64), (4, 2, 64)).reshape(1, 512)

    lines = [jnp.asarray(table) for table in line_tables()]
    grid, window = grid.reshape(256, SLOTS, 128), window.reshape(1024, 128)
    partial = line_call(me_near - me_near % 4, grid, lines, window, weight)
    parts = lax.all_to_all(partial.reshape(band_count, 32, ROWS), BAND, 0, 0, tiled=True)
    found = pick_call(parts, rows)
    found = lax.all_to_all(found, FFT, 0, 0, tiled=True)
    result = place_call(found, place).reshape(2, COL_DEV, waves)
    args = (valence_store, valence_energy, conduction, conduction_energy, sphere_map, owner)
    return lax.cond(fits, lambda *_: result, general_path, *args)


def broadcast(value, axis, source):
    kept = jnp.where(lax.axis_index(axis) == source, value, 0).astype(value.dtype)
    return lax.psum(kept, axis)


def dft_table(length):
    steps_n = lax.broadcasted_iota(jnp.int32, (length, length), 0)
    steps_k = lax.broadcasted_iota(jnp.int32, (length, length), 1)
    phase_angle = 2.0 * math.pi / length * (steps_n * steps_k % length).astype(jnp.float32)
    factor = 1.0 / math.sqrt(length)
    cosine = jnp.cos(phase_angle) * factor
    sine_part = jnp.sin(phase_angle) * factor
    upper_half = jnp.stack([cosine, -sine_part], axis=1)
    lower_half = jnp.stack([sine_part, cosine], axis=1)
    return jnp.stack([upper_half, lower_half], axis=0).astype(jnp.bfloat16)


def pair_products(valence, conduction):
    length = valence.shape[-1] // 2
    val_re = valence[..., :length].astype(jnp.float32)[:, None]
    val_im = valence[..., length:].astype(jnp.float32)[:, None]
    con_re = conduction[..., :length].astype(jnp.float32)[None]
    con_im = conduction[..., length:].astype(jnp.float32)[None]
    real_part = val_re * con_re + val_im * con_im
    imag_part = val_re * con_im - val_im * con_re
    joined = jnp.concatenate([real_part, imag_part], axis=-1).astype(jnp.bfloat16)
    return joined.reshape((-1,) + joined.shape[2:])


def along_z(values_in, twiddle):
    length = twiddle.shape[1]
    square = twiddle.reshape(2 * length, 2 * length)
    return jnp.dot(values_in, square, preferred_element_type=jnp.float32).astype(jnp.bfloat16)


def along_y(values_in, twiddle):
    length = twiddle.shape[1]
    split = values_in.reshape(values_in.shape[:3] + (2, length))
    mixed = jnp.einsum("axypz,pyqk->axkqz", split, twiddle, preferred_element_type=jnp.float32)
    return mixed.reshape(values_in.shape).astype(jnp.bfloat16)


def along_x(values_in, twiddle):
    length = twiddle.shape[1]
    split = values_in.reshape(values_in.shape[:3] + (2, length))
    mixed = jnp.einsum("axypz,pxqk->aqkyz", split, twiddle, preferred_element_type=jnp.float32)
    return mixed.astype(jnp.bfloat16)


def window_matrix(window, weights):
    scaled_re = (weights[:, None] * window[:, 0, :].astype(jnp.float32)).T
    scaled_im = (weights[:, None] * window[:, 1, :].astype(jnp.float32)).T
    first_row = jnp.stack([scaled_re, scaled_im], axis=2)
    second_row = jnp.stack([-scaled_im, scaled_re], axis=2)
    joined = jnp.stack([first_row, second_row], axis=0).astype(jnp.bfloat16)
    return joined.reshape(2 * joined.shape[1], 2 * joined.shape[2])


def general_path(valence_store, valence_energy, conduction, conduction_energy, sphere_map, owner):
    band_count = lax.axis_size(BAND)
    conduction_dev = conduction.shape[0]
    valence_total = valence_store.shape[1]
    length = conduction.shape[2]
    norm_scale = 1.0 / math.sqrt(valence_total * conduction_dev * band_count)
    twiddle = dft_table(length)
    window_total = COL_DEV * band_count
    slot_index = owner[0] % band_count
    valence = broadcast(valence_store, BAND, slot_index)[0]
    pair_grid = along_y(along_z(pair_products(valence, conduction), twiddle), twiddle)
    weights = (4.0 * norm_scale / (valence_energy[:, None] - conduction_energy[None, :])).reshape(
        -1
    )
    whole_grids = lax.all_to_all(pair_grid, FFT, split_axis=0, concat_axis=1, tiled=True)
    spectrum = along_x(whole_grids, twiddle)
    flat_grid = spectrum.reshape(spectrum.shape[0], 2, -1)
    sphere = jnp.take(flat_grid, sphere_map, axis=2)
    row_block = lax.all_to_all(sphere, FFT, split_axis=2, concat_axis=0, tiled=True)
    window = lax.all_gather(sphere[:, :, :window_total], FFT, axis=0, tiled=True)
    left_side = window_matrix(window, weights)
    right_side = row_block.reshape(-1, row_block.shape[2])
    product = jnp.dot(left_side, right_side, preferred_element_type=jnp.float32)
    partial_value = product.reshape(2, window_total, -1)
    return lax.psum_scatter(partial_value, BAND, scatter_dimension=1, tiled=True)


def solution(mesh):
    placed = (
        P(BAND, None, FFT, None, None),
        P(),
        P(BAND, FFT, None, None),
        P(BAND),
        P(),
        P(),
    )
    fine = Mesh(mesh.devices.reshape(tuple(AXES.values())), tuple(AXES))
    return jax.shard_map(
        on_device, mesh=fine, in_specs=placed, out_specs=P(None, BAND, FFT), check_vma=False
    )
```

```python
import functools
import math

import jax
import jax.numpy as jnp
import numpy as np
from jax import lax
from jax.experimental import pallas as pl
from jax.experimental.pallas import tpu as pltpu
from jax.sharding import Mesh
from jax.sharding import PartitionSpec as P

COL_DEV = 16
f32 = jnp.float32
bf16 = jnp.bfloat16

LENGTH = 64
RADIUS_SQ = 290
QUADS = sorted(
    (a * a + b * b, a, b)
    for a in range(18)
    for b in range(18)
    if a * a + b * b <= RADIUS_SQ and (a > 0 or b == 0)
)
GROUPS = 16
SLOTS = 16
USED = -(-len(QUADS) // GROUPS)
HEIGHT = [int(math.isqrt(RADIUS_SQ - QUADS[GROUPS * s][0])) for s in range(USED)]
BASE = [sum(2 * h + 1 for h in HEIGHT[:s]) for s in range(USED)]
ROWS = 384
CELLS = 4 * ROWS
CAP = 128
assert USED < SLOTS and BASE[-1] + 2 * HEIGHT[-1] + 1 <= ROWS

AXES = {"y": 4, "zl": 2, "c": 2, "x": 4, "zh": 4}
BAND = ("y", "zl", "c")
FFT = ("x", "zh")
NEAR = ("zl", "c", "x", "zh")


def unit_table(rows, columns):
    angle = 2.0 * np.pi / LENGTH * (np.outer(rows, columns) % LENGTH)
    cosine = (np.cos(angle) / 8.0).astype(np.float32).astype(jnp.bfloat16)
    sine = (np.sin(angle) / 8.0).astype(np.float32).astype(jnp.bfloat16)
    return cosine.astype(np.float32), sine.astype(np.float32)


def plane_table():
    cosine, sine = unit_table(np.arange(18), np.arange(LENGTH))
    table = np.zeros((4, 4, 4, SLOTS, LENGTH, LENGTH), np.float32)
    for index, (_, a, b) in enumerate(QUADS):
        g, s = index % GROUPS, index // GROUPS
        if b == 0 and a > 0:
            first, second = np.outer(cosine[a], cosine[0]), np.outer(cosine[0], cosine[a])
            turned, across = np.outer(sine[a], cosine[0]), np.outer(cosine[0], sine[a])
            kinds = (first + second, turned - across, turned + across, second - first)
            kinds = [0.5 * kind for kind in kinds]
        else:
            kinds = (
                np.outer(cosine[a], cosine[b]),
                np.outer(cosine[a], sine[b]),
                np.outer(sine[a], cosine[b]),
                np.outer(sine[a], sine[b]),
            )
        for kind in range(4):
            table[g // 4, kind, g % 4, s] = kinds[kind]
    return table.reshape(GROUPS * 4 * SLOTS, LENGTH * LENGTH).astype(jnp.bfloat16)


def line_tables():
    cosine, sine = unit_table(np.arange(24), np.arange(LENGTH))
    return [
        np.concatenate([cosine[:n], sine[:n]], axis=0).astype(jnp.bfloat16) for n in (8, 16, 24)
    ]


def lookup_table():
    table = np.zeros((4, 18, 18), np.float32)
    for index, (_, a, b) in enumerate(QUADS):
        s = index // GROUPS
        table[:, a, b] = (index, BASE[s] // 16, BASE[s] % 16, HEIGHT[s])
        if b == 0:
            table[:, 0, a] = table[:, a, b]
    return table


def swap(value):
    lane = lax.broadcasted_iota(jnp.int32, value.shape, 1)
    turned = pltpu.roll(value, 64, 1)
    return jnp.where(lane < 64, turned, -turned)


def route_kernel(map_ref, table_ref, out_ref):
    out_ref[...] = jnp.zeros_like(out_ref)
    step = lax.broadcasted_iota(jnp.int32, (32, 2048), 0)
    for n in range(0, map_ref.shape[1], 2048):
        lanes = slice(n, n + 2048)
        cell = map_ref[:, lanes]
        coords = (cell >> 12, (cell >> 6) & 63, cell & 63)
        kx, ky, kz = (jnp.where(coord < 32, coord, coord - 64) for coord in coords)
        inside = kx * kx + ky * ky + kz * kz <= RADIUS_SQ
        hot_y = jnp.where(step == jnp.abs(ky), 1.0, 0.0).astype(bf16)
        hot_z = jnp.where(step == jnp.abs(kz), 1.0, 0.0)
        found = jnp.dot(table_ref[...], hot_y, preferred_element_type=f32)
        found = [
            jnp.sum(found[32 * i : 32 * i + 32] * hot_z, axis=0, keepdims=True).astype(jnp.int32)
            for i in range(4)
        ]
        quad, base, height = found[0], found[1] * 16 + found[2], found[3]
        group, slot = quad & (GROUPS - 1), quad >> 4
        variant = jnp.where(ky < 0, 2, 0) + jnp.where(kz < 0, 1, 0)
        variant = jnp.where(kz == 0, jnp.where(ky < 0, 3, 0), variant)
        variant = jnp.where((ky == 0) & (kz != 0), jnp.where(kz < 0, 2, 1), variant)
        out_ref[0:1, lanes] = group
        row = variant * ROWS + base + jnp.where(kx >= 0, kx, height - kx)
        out_ref[1:2, lanes] = row
        out_ref[2:3, lanes] = jnp.where(inside, 1, 0)


def window_kernel(cell_ref, unit_ref, out_ref):
    cell = cell_ref[...]
    step = lax.broadcasted_iota(jnp.int32, (256, 32), 1)
    lane = lax.broadcasted_iota(jnp.int32, (256, 128), 1)
    units = []
    for coord in ((cell >> 6) & 63, cell & 63):
        freq = jnp.where(coord < 32, coord, coord - 64)
        hot = jnp.where(step == jnp.abs(freq), 1.0, 0.0).astype(bf16)
        unit = jnp.dot(hot, unit_ref[...], preferred_element_type=f32)
        units.append(jnp.where((lane >= 64) & (freq < 0), -unit, unit))
    along_y, along_z = units
    turned = pltpu.roll(along_z, 64, 1)
    cos_z = jnp.where(lane < 64, along_z, turned)
    sin_z = jnp.where(lane < 64, turned, along_z)
    for y in range(0, LENGTH, 2):
        cos_y = jnp.where(lane < 64, along_y[:, y : y + 1], along_y[:, y + 1 : y + 2])
        sin_y = jnp.where(lane < 64, along_y[:, 64 + y : 65 + y], along_y[:, 65 + y : 66 + y])
        lanes = slice(y * 64, y * 64 + 128)
        out_ref[:256, lanes] = (cos_y * cos_z - sin_y * sin_z).astype(bf16)
        out_ref[256:, lanes] = (sin_y * cos_z + cos_y * sin_z).astype(bf16)


def window_call(cells):
    unit = np.concatenate(unit_table(np.arange(32), np.arange(LENGTH)), axis=1)
    return pl.pallas_call(
        window_kernel,
        out_shape=jax.ShapeDtypeStruct((512, 4096), bf16),
        compiler_params=pltpu.CompilerParams(vmem_limit_bytes=16 * 1024 * 1024),
        cost_estimate=pl.CostEstimate(
            flops=16 * 512 * 4096, bytes_accessed=4 << 20, transcendentals=0
        ),
    )(cells.reshape(256, 1), jnp.asarray(unit, bf16))


def route(sphere_map):
    waves = sphere_map.shape[0]
    table = np.zeros((4, 32, 32), np.float32)
    table[:, :18, :18] = lookup_table().transpose(0, 2, 1)
    return pl.pallas_call(
        route_kernel,
        out_shape=jax.ShapeDtypeStruct((8, waves), jnp.int32),
        compiler_params=pltpu.CompilerParams(vmem_limit_bytes=8 * 1024 * 1024),
        cost_estimate=pl.CostEstimate(
            flops=2 * 128 * 32 * waves, bytes_accessed=40 * waves, transcendentals=0
        ),
    )(sphere_map.reshape(1, waves), jnp.asarray(table.reshape(128, 32), bf16))


def pair_kernel(
    first_ref,
    second_ref,
    con_ref,
    table_ref,
    turn_ref,
    pair_ref,
    part_ref,
    wide_ref,
    val_ref,
    buffer_ref,
    sem_ref,
):
    copy = pltpu.make_async_copy(table_ref, buffer_ref, sem_ref)
    copy.start()
    for band in range(2):
        for x in range(4):
            start = (band * 4 + x) * 64
            wide_ref[start : start + 64, :] = first_ref[band, x].astype(f32)
            wide_ref[512 + start : 576 + start, :] = second_ref[band, x].astype(f32)
    left = lax.broadcasted_iota(jnp.int32, (4, 128), 1) < 64

    for y in range(0, LENGTH, 2):
        lanes = slice(y * 64, y * 64 + 128)
        for x in range(4):
            even = wide_ref[pl.ds(x * 64 + y, 4, stride=256), :]
            odd = wide_ref[pl.ds(x * 64 + y + 1, 4, stride=256), :]
            val_ref[2 * x, :, lanes] = jnp.where(left, even, pltpu.roll(odd, 64, 1))
            val_ref[2 * x + 1, :, lanes] = jnp.where(left, pltpu.roll(even, 64, 1), odd)

    chunk = 512

    @pl.loop(0, LENGTH * LENGTH // chunk)
    def _(k):
        lanes = pl.ds(pl.multiple_of(k * chunk, chunk), chunk)
        for x in range(4):
            con_re = con_ref[2 * x, :, lanes].astype(f32)
            con_im = con_ref[2 * x + 1, :, lanes].astype(f32)
            for v in range(4):
                val_re = val_ref[2 * x, pl.ds(v, 1), lanes]
                val_im = val_ref[2 * x + 1, pl.ds(v, 1), lanes]
                real = val_re * con_re + val_im * con_im
                imag = val_re * con_im - val_im * con_re
                pair_ref[pl.ds(x * 128 + v * 16, 16), lanes] = real.astype(bf16)
                pair_ref[pl.ds(x * 128 + 64 + v * 16, 16), lanes] = imag.astype(bf16)

    copy.wait()
    total = jnp.zeros(part_ref.shape, f32)
    for x in range(4):
        mixed = lax.dot_general(
            buffer_ref[...],
            pair_ref[x * 128 : (x + 1) * 128, :],
            (((1,), (1,)), ((), ())),
            preferred_element_type=f32,
        )
        value = mixed[:256] + swap(mixed[256:])
        total += turn_ref[:, x : x + 1] * value
        total += swap(turn_ref[:, 4 + x : 5 + x] * value)
    part_ref[...] = total


def pair_call(first, second, con, table, turn):
    whole = pl.BlockSpec(memory_space=pltpu.VMEM)
    table = pltpu.with_memory_space_constraint(table, pltpu.HBM)
    return pl.pallas_call(
        pair_kernel,
        in_specs=[whole] * 3 + [pl.BlockSpec(memory_space=pltpu.HBM), whole],
        out_shape=[
            pltpu.VMEM((512, 4096), bf16),
            jax.ShapeDtypeStruct((256, 128), f32),
        ],
        scratch_shapes=[
            pltpu.VMEM((1024, 128), f32),
            pltpu.VMEM((8, 4, 4096), f32),
            pltpu.VMEM((512, 4096), bf16),
            pltpu.SemaphoreType.DMA,
        ],
        compiler_params=pltpu.CompilerParams(vmem_limit_bytes=22 * 1024 * 1024),
        cost_estimate=pl.CostEstimate(
            flops=2 * 512 * 512 * 4096, bytes_accessed=10 << 20, transcendentals=0
        ),
    )(first, second, con, table, turn)


def plane_kernel(pair_ref, table_ref, send_ref, buffer_ref, sem_ref):
    copies = [
        pltpu.make_async_copy(
            table_ref.at[pl.ds(i * 256, 256)], buffer_ref.at[i], sem_ref.at[i]
        )
        for i in range(4)
    ]
    for copy in copies:
        copy.start()
    for i in range(4):
        copies[i].wait()
        mixed = lax.dot_general(
            buffer_ref[i], pair_ref[...], (((1,), (1,)), ((), ())), preferred_element_type=f32
        )
        for x in range(4):
            part = mixed[:, x * 128 : (x + 1) * 128]
            cc, cs, sc, ss = (part[64 * k : 64 * (k + 1)] for k in range(4))
            sc, cs = swap(sc), swap(cs)
            same, other = cc - ss, cc + ss
            total, apart = sc + cs, sc - cs
            signs = (same + total, other + apart, other - apart, same - total)
            columns = jnp.concatenate([value.astype(bf16) for value in signs], axis=0)
            send_ref[:, 4 * i : 4 * i + 4, x] = columns.reshape(4, 4, SLOTS, 128)


def plane_call(pairs, table):
    return pl.pallas_call(
        plane_kernel,
        in_specs=[
            pl.BlockSpec(memory_space=pltpu.VMEM),
            pl.BlockSpec(memory_space=pltpu.HBM),
        ],
        out_shape=jax.ShapeDtypeStruct((4, GROUPS, 4, SLOTS, 128), bf16),
        scratch_shapes=[pltpu.VMEM((4, 256, 4096), bf16), pltpu.SemaphoreType.DMA((4,))],
        compiler_params=pltpu.CompilerParams(vmem_limit_bytes=24 * 1024 * 1024),
        cost_estimate=pl.CostEstimate(
            flops=2 * 1024 * 512 * 4096, bytes_accessed=8 << 20, transcendentals=0
        ),
    )(pairs, pltpu.with_memory_space_constraint(table, pltpu.HBM))


def line_kernel(
    me_ref,
    grid_ref,
    line8_ref,
    line16_ref,
    line24_ref,
    window_ref,
    weight_ref,
    out_ref,
    wide_ref,
    rho_ref,
    left_ref,
):
    lines = {8: line8_ref, 16: line16_ref, 24: line24_ref}

    @pl.loop(0, 4 * LENGTH, step=4)
    def _(x):
        for i in range(4):
            start = pl.multiple_of((x + i) * SLOTS, SLOTS)
            wide_ref[pl.ds(start, SLOTS), :] = grid_ref[x + i].astype(f32)

    last = BASE[-1] + 2 * HEIGHT[-1] + 1
    rho_ref[last - last % 8 :, :] = jnp.zeros((ROWS - last + last % 8, 512), f32)
    for slot in range(USED):
        lane_tiles = [
            wide_ref[pl.ds(q * LENGTH * SLOTS + slot, LENGTH, stride=SLOTS), :] for q in range(4)
        ]
        values = jnp.concatenate(lane_tiles, axis=1).astype(bf16)
        count, base = HEIGHT[slot] + 1, BASE[slot]
        rows = -(-count // 8) * 8
        mixed = jnp.dot(lines[rows][...], values, preferred_element_type=f32)
        for q in range(4):
            lanes = slice(q * 128, (q + 1) * 128)
            cosine, sine = mixed[:rows, lanes], swap(mixed[rows:, lanes])
            rho_ref[base + count - 1 : base + 2 * count - 1, lanes] = (cosine - sine)[:count]
            rho_ref[base : base + count, lanes] = (cosine + sine)[:count]

    me = me_ref[0]
    wave = lax.broadcasted_iota(jnp.int32, (256, 1024), 0)
    column = lax.broadcasted_iota(jnp.int32, (256, 1024), 1)
    for q in range(4):
        lanes = slice(q * 128, (q + 1) * 128)
        place = ((q * 16 + wave // 16) ^ me) * 16 + wave % 16
        order = jnp.where(column == place, 1.0, 0.0).astype(bf16)
        values = jnp.dot(order, window_ref[...], preferred_element_type=f32)
        scaled = (weight_ref[:, lanes] * values).astype(bf16).astype(f32)
        turned = -swap(scaled)
        for b in range(COL_DEV):
            left_ref[b * 32 : b * 32 + 16, lanes] = scaled[b * 16 : b * 16 + 16].astype(bf16)
            left_ref[b * 32 + 16 : b * 32 + 32, lanes] = turned[b * 16 : b * 16 + 16].astype(bf16)
    for n in range(0, ROWS, 128):
        product = lax.dot_general(
            left_ref[...],
            rho_ref[n : n + 128, :].astype(bf16),
            (((1,), (1,)), ((), ())),
            preferred_element_type=f32,
        )
        out_ref[:, n : n + 128] = product.astype(bf16)


def line_call(me, grid, lines, window, weight):
    whole = pl.BlockSpec(memory_space=pltpu.VMEM)
    return pl.pallas_call(
        line_kernel,
        in_specs=[pl.BlockSpec(memory_space=pltpu.SMEM)] + [whole] * 6,
        out_shape=jax.ShapeDtypeStruct((512, ROWS), bf16),
        scratch_shapes=[
            pltpu.VMEM((4 * LENGTH * SLOTS, 128), f32),
            pltpu.VMEM((ROWS, 512), f32),
            pltpu.VMEM((512, 512), bf16),
        ],
        compiler_params=pltpu.CompilerParams(vmem_limit_bytes=16 * 1024 * 1024),
        cost_estimate=pl.CostEstimate(
            flops=2 * 512 * 512 * ROWS, bytes_accessed=3 << 20, transcendentals=0
        ),
    )(me.reshape(1), grid, *lines, window, weight)


def split(value):
    high = value.astype(bf16)
    return high, (value - high.astype(f32)).astype(bf16)


def pick_kernel(parts_ref, rows_ref, out_ref, both_ref):
    for q in range(4):
        lanes = slice(q * ROWS, (q + 1) * ROWS)
        total = parts_ref[q].astype(f32)
        for y in range(1, 4):
            total += parts_ref[4 * y + q].astype(f32)
        both_ref[:32, lanes], both_ref[32:, lanes] = split(total)
    for n in range(0, 16 * CAP, 256):
        cell = lax.broadcasted_iota(jnp.int32, (CELLS, 256), 0)
        chosen = jnp.where(cell == rows_ref[:, n : n + 256], 1.0, 0.0).astype(bf16)
        found = jnp.dot(both_ref[...], chosen, preferred_element_type=f32)
        found = found[:32] + found[32:]
        for i in range(256 // CAP):
            out_ref[n // CAP + i] = found[:, i * CAP : (i + 1) * CAP]


def pick_call(parts, rows):
    return pl.pallas_call(
        pick_kernel,
        out_shape=jax.ShapeDtypeStruct((16, 32, CAP), f32),
        scratch_shapes=[pltpu.VMEM((64, CELLS), bf16)],
        compiler_params=pltpu.CompilerParams(vmem_limit_bytes=16 * 1024 * 1024),
        cost_estimate=pl.CostEstimate(
            flops=2 * 64 * CELLS * 16 * CAP, bytes_accessed=2 << 20, transcendentals=0
        ),
    )(parts, rows)


def place_kernel(found_ref, place_ref, out_ref, both_ref):
    for i in range(16):
        both_ref[:32, i * CAP : (i + 1) * CAP], both_ref[32:, i * CAP : (i + 1) * CAP] = split(
            found_ref[i]
        )
    for n in range(0, out_ref.shape[1], 256):
        slot = lax.broadcasted_iota(jnp.int32, (16 * CAP, 256), 0)
        chosen = jnp.where(slot == place_ref[:, n : n + 256], 1.0, 0.0).astype(bf16)
        value = jnp.dot(both_ref[...], chosen, preferred_element_type=f32)
        out_ref[:, n : n + 256] = value[:32] + value[32:]


def place_call(found, place):
    return pl.pallas_call(
        place_kernel,
        out_shape=jax.ShapeDtypeStruct((32, place.shape[1]), f32),
        scratch_shapes=[pltpu.VMEM((64, 16 * CAP), bf16)],
        compiler_params=pltpu.CompilerParams(vmem_limit_bytes=16 * 1024 * 1024),
        cost_estimate=pl.CostEstimate(
            flops=2 * 64 * 16 * CAP * 1280, bytes_accessed=1 << 20, transcendentals=0
        ),
    )(found, place)


def block(value, index):
    return lax.dynamic_index_in_dim(value, index, 0, keepdims=False)


def far(value, axis, step):
    size = math.prod(AXES[name] for name in (axis if isinstance(axis, tuple) else (axis,)))
    return lax.ppermute(value, axis, [(i, i ^ step) for i in range(size)])


def scatter_inputs(store, con, slot_index, sphere_map):
    y, zl, c = (lax.axis_index(name) for name in BAND)
    from_y, from_zl, from_c = slot_index // 4, slot_index // 2 % 2, slot_index % 2
    other = far(block(store, 1 - c), "c", 1)
    held = jnp.where(c == from_c, block(store, c), other)

    def along_rows(value):
        sent = [block(value, y ^ step) for step in range(1, 4)]
        got = [far(sent[step - 1], "y", step) for step in range(1, 4)]
        mine = block(value, y)
        for step in range(1, 4):
            mine = jnp.where(y ^ from_y == step, got[step - 1], mine)
        return mine, sent

    def along_pairs(value):
        return jnp.where(zl == from_zl, block(value, zl), far(block(value, 1 - zl), "zl", 1))

    later = held[:, :, 2:].swapaxes(0, 1)
    first, sent = along_rows(held[:, :, :2])
    con = lax.optimization_barrier((con, sent, block(later, 1 - zl)))[0]
    rows = jnp.stack([con] + [far(con, "y", step) for step in range(1, 4)])
    sphere_map = lax.optimization_barrier((sphere_map, rows))[0]
    pairs = jnp.stack([rows, far(rows, "zl", 1)], axis=1)
    both = jnp.stack([pairs, far(pairs, "c", 1)], axis=2)
    first = along_pairs(first)
    second = along_rows(along_pairs(later))[0]
    return first, second, both.reshape((16,) + con.shape), sphere_map


def window_and_planes(pairs, part, table):
    x = lax.axis_index("x")
    part = part.reshape(4, 4, 16, 128)
    got = [block(part, x)] + [far(block(part, x ^ step), "x", step) for step in range(1, 4)]
    planes = plane_call(pairs, table)
    got, planes = lax.optimization_barrier((got, planes))
    total = got[0] + got[1] + got[2] + got[3]
    got = [far(total, "zh", step) for step in range(1, 4)]
    got[0], planes = lax.optimization_barrier((got[0], planes))
    return (total + got[0] + got[1] + got[2]).astype(bf16), planes


def gather_window(value):
    value = jnp.stack([value] + [far(value, "x", step) for step in range(1, 4)])
    return jnp.stack([value] + [far(value, ("zl", "c"), step) for step in range(1, 4)])


def on_device(valence_store, valence_energy, conduction, conduction_energy, sphere_map, owner):
    band_count, fft_count = lax.axis_size(BAND), lax.axis_size(FFT)
    me_band, me_fft, me_near = (lax.axis_index(axis) for axis in (BAND, FFT, NEAR))
    valence_total = valence_store.shape[1]
    conduction_total = conduction.shape[0] * band_count
    window_total = COL_DEV * band_count
    share = valence_total // band_count
    waves = sphere_map.shape[0] // fft_count

    con = conduction.reshape(4, 64, 2, 64).transpose(0, 2, 1, 3).reshape(8, 4096)
    energy, pieces = conduction_energy[0], []
    for _ in range(3):
        pieces.append(lax.reduce_precision(energy, 8, 7))
        energy = energy - pieces[-1]
    extra = jnp.zeros((8, 128), f32).at[0, :3].set(jnp.stack(pieces)).astype(bf16)
    con = jnp.concatenate([con, extra], axis=1)
    store = valence_store.reshape((2, 4, 2, share) + valence_store.shape[2:])
    slot_index = owner[0] % band_count
    first, second, con, sphere_map = scatter_inputs(store, con, slot_index, sphere_map)
    energies = jnp.sum(con[:, 0, 4096:4099].astype(f32), axis=1)
    con = con[:, :, :4096].transpose(1, 0, 2)

    window_cells = sphere_map[:window_total]
    window_table = window_call(window_cells)
    kx = (window_cells // 4096)[:, None]
    x_here = 4 * me_fft + jnp.arange(4, dtype=jnp.int32)
    angle = 2.0 * math.pi / 64 * ((kx * x_here[None]) % 64).astype(f32)
    turn = jnp.concatenate([jnp.cos(angle) / 8.0, jnp.sin(angle) / 8.0], axis=1)
    turn = turn.astype(bf16).astype(f32)

    pairs, part = pair_call(first, second, con, window_table, turn)
    part, planes = window_and_planes(pairs, part, jnp.asarray(plane_table()))
    window = gather_window(part)
    sphere_map = lax.optimization_barrier((sphere_map, planes))[0]

    routed = route(sphere_map)
    by_block = routed[0].reshape(fft_count, waves)
    devices = jnp.arange(fft_count, dtype=jnp.int32)
    counts = jnp.sum(
        (by_block[:, None, :] == devices[None, :, None]).astype(jnp.int32), axis=2
    )
    fits = jnp.all(routed[2] == 1) & jnp.all(counts <= CAP)
    mine = by_block == me_fft
    own_block = lax.dynamic_index_in_dim(by_block, me_fft, 0, keepdims=False)
    from_device = own_block[None] == devices[:, None]
    masks = jnp.concatenate([mine, from_device], axis=0).astype(bf16)
    before = lax.broadcasted_iota(jnp.int32, (waves, waves), 0)
    upto = lax.broadcasted_iota(jnp.int32, (waves, waves), 1)
    order = jnp.dot(masks, (before <= upto).astype(bf16), preferred_element_type=f32)
    order = order.astype(jnp.int32) - 1
    slots = jnp.arange(CAP, dtype=jnp.int32)
    chosen = mine[:, :, None] & (order[:fft_count, :, None] == slots)
    row_block = routed[1].reshape(fft_count, waves)
    halves = jnp.stack([row_block // 64, row_block % 64], axis=1).astype(bf16)
    listed = jnp.einsum(
        "fpg,fgs->fps", halves, chosen.astype(bf16), preferred_element_type=f32
    ).astype(jnp.int32)
    rows = (listed[:, 0] * 64 + listed[:, 1]).reshape(1, fft_count * CAP)
    rank = jnp.sum(jnp.where(from_device, order[fft_count:], 0), axis=0)
    place = (own_block * CAP + rank).reshape(1, waves)
    grid = lax.all_to_all(planes.reshape(64, 4, SLOTS, 128), NEAR, 0, 0, tiled=True)
    norm_scale = 1.0 / math.sqrt(valence_total * conduction_total)
    near = jnp.arange(4, dtype=jnp.int32)
    bands = (near % 2) * 8 + lax.axis_index("y") * 2 + near // 2
    hot = bands[:, None, None] == (jnp.arange(valence_total) // share)[None, None, :]
    hot = hot & (jnp.arange(share)[None, :, None] == (jnp.arange(valence_total) % share))
    near_valence = jnp.sum(jnp.where(hot, valence_energy, 0.0), axis=2)
    steps = jnp.arange(band_count, dtype=jnp.int32)
    places = (near ^ (me_band % 4))[:, None] ^ steps[None, :]
    near_conduction = jnp.sum(
        jnp.where(places[:, :, None] == steps[None, None, :], energies, 0.0), axis=2
    )
    weight = 4.0 * norm_scale / (near_valence[:, :, None] - near_conduction[:, None, :])
    weight = jnp.broadcast_to(weight.reshape(4, 1, 64), (4, 2, 64)).reshape(1, 512)

    lines = [jnp.asarray(table) for table in line_tables()]
    grid, window = grid.reshape(256, SLOTS, 128), window.reshape(1024, 128)
    partial = line_call(me_near - me_near % 4, grid, lines, window, weight)
    parts = lax.all_to_all(partial.reshape(band_count, 32, ROWS), BAND, 0, 0, tiled=True)
    found = pick_call(parts, rows)
    found = lax.all_to_all(found, FFT, 0, 0, tiled=True)
    result = place_call(found, place).reshape(2, COL_DEV, waves)
    args = (valence_store, valence_energy, conduction, conduction_energy, sphere_map, owner)
    return lax.cond(fits, lambda *_: result, general_path, *args)


def broadcast(value, axis, source):
    kept = jnp.where(lax.axis_index(axis) == source, value, 0).astype(value.dtype)
    return lax.psum(kept, axis)


def dft_table(length):
    steps_n = lax.broadcasted_iota(jnp.int32, (length, length), 0)
    steps_k = lax.broadcasted_iota(jnp.int32, (length, length), 1)
    phase_angle = 2.0 * math.pi / length * (steps_n * steps_k % length).astype(jnp.float32)
    factor = 1.0 / math.sqrt(length)
    cosine = jnp.cos(phase_angle) * factor
    sine_part = jnp.sin(phase_angle) * factor
    upper_half = jnp.stack([cosine, -sine_part], axis=1)
    lower_half = jnp.stack([sine_part, cosine], axis=1)
    return jnp.stack([upper_half, lower_half], axis=0).astype(jnp.bfloat16)


def pair_products(valence, conduction):
    length = valence.shape[-1] // 2
    val_re = valence[..., :length].astype(jnp.float32)[:, None]
    val_im = valence[..., length:].astype(jnp.float32)[:, None]
    con_re = conduction[..., :length].astype(jnp.float32)[None]
    con_im = conduction[..., length:].astype(jnp.float32)[None]
    real_part = val_re * con_re + val_im * con_im
    imag_part = val_re * con_im - val_im * con_re
    joined = jnp.concatenate([real_part, imag_part], axis=-1).astype(jnp.bfloat16)
    return joined.reshape((-1,) + joined.shape[2:])


def along_z(values_in, twiddle):
    length = twiddle.shape[1]
    square = twiddle.reshape(2 * length, 2 * length)
    return jnp.dot(values_in, square, preferred_element_type=jnp.float32).astype(jnp.bfloat16)


def along_y(values_in, twiddle):
    length = twiddle.shape[1]
    split = values_in.reshape(values_in.shape[:3] + (2, length))
    mixed = jnp.einsum("axypz,pyqk->axkqz", split, twiddle, preferred_element_type=jnp.float32)
    return mixed.reshape(values_in.shape).astype(jnp.bfloat16)


def along_x(values_in, twiddle):
    length = twiddle.shape[1]
    split = values_in.reshape(values_in.shape[:3] + (2, length))
    mixed = jnp.einsum("axypz,pxqk->aqkyz", split, twiddle, preferred_element_type=jnp.float32)
    return mixed.astype(jnp.bfloat16)


def window_matrix(window, weights):
    scaled_re = (weights[:, None] * window[:, 0, :].astype(jnp.float32)).T
    scaled_im = (weights[:, None] * window[:, 1, :].astype(jnp.float32)).T
    first_row = jnp.stack([scaled_re, scaled_im], axis=2)
    second_row = jnp.stack([-scaled_im, scaled_re], axis=2)
    joined = jnp.stack([first_row, second_row], axis=0).astype(jnp.bfloat16)
    return joined.reshape(2 * joined.shape[1], 2 * joined.shape[2])


def general_path(valence_store, valence_energy, conduction, conduction_energy, sphere_map, owner):
    band_count = lax.axis_size(BAND)
    conduction_dev = conduction.shape[0]
    valence_total = valence_store.shape[1]
    length = conduction.shape[2]
    norm_scale = 1.0 / math.sqrt(valence_total * conduction_dev * band_count)
    twiddle = dft_table(length)
    window_total = COL_DEV * band_count
    slot_index = owner[0] % band_count
    valence = broadcast(valence_store, BAND, slot_index)[0]
    pair_grid = along_y(along_z(pair_products(valence, conduction), twiddle), twiddle)
    weights = (4.0 * norm_scale / (valence_energy[:, None] - conduction_energy[None, :])).reshape(
        -1
    )
    whole_grids = lax.all_to_all(pair_grid, FFT, split_axis=0, concat_axis=1, tiled=True)
    spectrum = along_x(whole_grids, twiddle)
    flat_grid = spectrum.reshape(spectrum.shape[0], 2, -1)
    sphere = jnp.take(flat_grid, sphere_map, axis=2)
    row_block = lax.all_to_all(sphere, FFT, split_axis=2, concat_axis=0, tiled=True)
    window = lax.all_gather(sphere[:, :, :window_total], FFT, axis=0, tiled=True)
    left_side = window_matrix(window, weights)
    right_side = row_block.reshape(-1, row_block.shape[2])
    product = jnp.dot(left_side, right_side, preferred_element_type=jnp.float32)
    partial_value = product.reshape(2, window_total, -1)
    return lax.psum_scatter(partial_value, BAND, scatter_dimension=1, tiled=True)


def solution(mesh):
    placed = (
        P(BAND, None, FFT, None, None),
        P(),
        P(BAND, FFT, None, None),
        P(BAND),
        P(),
        P(),
    )
    fine = Mesh(mesh.devices.reshape(tuple(AXES.values())), tuple(AXES))
    return jax.shard_map(
        on_device, mesh=fine, in_specs=placed, out_specs=P(None, BAND, FFT), check_vma=False
    )
```

```python
import functools
import math

import jax
import jax.numpy as jnp
import numpy as np
from jax import lax
from jax.experimental import pallas as pl
from jax.experimental.pallas import tpu as pltpu
from jax.sharding import Mesh
from jax.sharding import PartitionSpec as P

COL_DEV = 16
f32 = jnp.float32
bf16 = jnp.bfloat16

LENGTH = 64
RADIUS_SQ = 290
QUADS = sorted(
    (a * a + b * b, a, b)
    for a in range(18)
    for b in range(18)
    if a * a + b * b <= RADIUS_SQ and (a > 0 or b == 0)
)
GROUPS = 16
SLOTS = 16
USED = -(-len(QUADS) // GROUPS)
HEIGHT = [int(math.isqrt(RADIUS_SQ - QUADS[GROUPS * s][0])) for s in range(USED)]
BASE = [sum(2 * h + 1 for h in HEIGHT[:s]) for s in range(USED)]
ROWS = 384
CELLS = 4 * ROWS
CAP = 128
assert USED < SLOTS and BASE[-1] + 2 * HEIGHT[-1] + 1 <= ROWS

AXES = {"y": 4, "zl": 2, "c": 2, "x": 4, "zh": 4}
BAND = ("y", "zl", "c")
FFT = ("x", "zh")
NEAR = ("zl", "c", "x", "zh")


def unit_table(rows, columns):
    angle = 2.0 * np.pi / LENGTH * (np.outer(rows, columns) % LENGTH)
    cosine = (np.cos(angle) / 8.0).astype(np.float32).astype(jnp.bfloat16)
    sine = (np.sin(angle) / 8.0).astype(np.float32).astype(jnp.bfloat16)
    return cosine.astype(np.float32), sine.astype(np.float32)


def plane_table():
    cosine, sine = unit_table(np.arange(18), np.arange(LENGTH))
    table = np.zeros((4, 4, 4, SLOTS, LENGTH, LENGTH), np.float32)
    for index, (_, a, b) in enumerate(QUADS):
        g, s = index % GROUPS, index // GROUPS
        if b == 0 and a > 0:
            first, second = np.outer(cosine[a], cosine[0]), np.outer(cosine[0], cosine[a])
            turned, across = np.outer(sine[a], cosine[0]), np.outer(cosine[0], sine[a])
            kinds = (first + second, turned - across, turned + across, second - first)
            kinds = [0.5 * kind for kind in kinds]
        else:
            kinds = (
                np.outer(cosine[a], cosine[b]),
                np.outer(cosine[a], sine[b]),
                np.outer(sine[a], cosine[b]),
                np.outer(sine[a], sine[b]),
            )
        for kind in range(4):
            table[g // 4, kind, g % 4, s] = kinds[kind]
    return table.reshape(GROUPS * 4 * SLOTS, LENGTH * LENGTH).astype(jnp.bfloat16)


def line_tables():
    cosine, sine = unit_table(np.arange(24), np.arange(LENGTH))
    return [
        np.concatenate([cosine[:n], sine[:n]], axis=0).astype(jnp.bfloat16) for n in (8, 16, 24)
    ]


def lookup_table():
    table = np.zeros((4, 18, 18), np.float32)
    for index, (_, a, b) in enumerate(QUADS):
        s = index // GROUPS
        table[:, a, b] = (index, BASE[s] // 16, BASE[s] % 16, HEIGHT[s])
        if b == 0:
            table[:, 0, a] = table[:, a, b]
    return table


def swap(value):
    lane = lax.broadcasted_iota(jnp.int32, value.shape, 1)
    turned = pltpu.roll(value, 64, 1)
    return jnp.where(lane < 64, turned, -turned)


def route_kernel(map_ref, table_ref, out_ref):
    out_ref[...] = jnp.zeros_like(out_ref)
    step = lax.broadcasted_iota(jnp.int32, (32, 2048), 0)
    for n in range(0, map_ref.shape[1], 2048):
        lanes = slice(n, n + 2048)
        cell = map_ref[:, lanes]
        coords = (cell >> 12, (cell >> 6) & 63, cell & 63)
        kx, ky, kz = (jnp.where(coord < 32, coord, coord - 64) for coord in coords)
        inside = kx * kx + ky * ky + kz * kz <= RADIUS_SQ
        hot_y = jnp.where(step == jnp.abs(ky), 1.0, 0.0).astype(bf16)
        hot_z = jnp.where(step == jnp.abs(kz), 1.0, 0.0)
        found = jnp.dot(table_ref[...], hot_y, preferred_element_type=f32)
        found = [
            jnp.sum(found[32 * i : 32 * i + 32] * hot_z, axis=0, keepdims=True).astype(jnp.int32)
            for i in range(4)
        ]
        quad, base, height = found[0], found[1] * 16 + found[2], found[3]
        group, slot = quad & (GROUPS - 1), quad >> 4
        variant = jnp.where(ky < 0, 2, 0) + jnp.where(kz < 0, 1, 0)
        variant = jnp.where(kz == 0, jnp.where(ky < 0, 3, 0), variant)
        variant = jnp.where((ky == 0) & (kz != 0), jnp.where(kz < 0, 2, 1), variant)
        out_ref[0:1, lanes] = group
        row = variant * ROWS + base + jnp.where(kx >= 0, kx, height - kx)
        out_ref[1:2, lanes] = row
        out_ref[2:3, lanes] = jnp.where(inside, 1, 0)


def window_kernel(cell_ref, unit_ref, done_ref, out_ref, sem_ref):
    copies = [
        pltpu.make_async_copy(
            out_ref.at[:, pl.ds(i * 1024, 1024)],
            done_ref.at[:, pl.ds(i * 1024, 1024)],
            sem_ref.at[i],
        )
        for i in range(4)
    ]
    cell = cell_ref[...]
    step = lax.broadcasted_iota(jnp.int32, (256, 32), 1)
    lane = lax.broadcasted_iota(jnp.int32, (256, 128), 1)
    units = []
    for coord in ((cell >> 6) & 63, cell & 63):
        freq = jnp.where(coord < 32, coord, coord - 64)
        hot = jnp.where(step == jnp.abs(freq), 1.0, 0.0).astype(bf16)
        unit = jnp.dot(hot, unit_ref[...], preferred_element_type=f32)
        units.append(jnp.where((lane >= 64) & (freq < 0), -unit, unit))
    along_y, along_z = units
    turned = pltpu.roll(along_z, 64, 1)
    cos_z = jnp.where(lane < 64, along_z, turned)
    sin_z = jnp.where(lane < 64, turned, along_z)
    for y in range(0, LENGTH, 2):
        cos_y = jnp.where(lane < 64, along_y[:, y : y + 1], along_y[:, y + 1 : y + 2])
        sin_y = jnp.where(lane < 64, along_y[:, 64 + y : 65 + y], along_y[:, 65 + y : 66 + y])
        lanes = slice(y * 64, y * 64 + 128)
        out_ref[:256, lanes] = (cos_y * cos_z - sin_y * sin_z).astype(bf16)
        out_ref[256:, lanes] = (sin_y * cos_z + cos_y * sin_z).astype(bf16)
        if y % 16 == 14:
            copies[y // 16].start()
    for copy in copies:
        copy.wait()


def window_call(cells):
    unit = np.concatenate(unit_table(np.arange(32), np.arange(LENGTH)), axis=1)
    return pl.pallas_call(
        window_kernel,
        out_shape=pltpu.HBM((512, 4096), bf16),
        out_specs=pl.BlockSpec(memory_space=pltpu.HBM),
        scratch_shapes=[pltpu.VMEM((512, 4096), bf16), pltpu.SemaphoreType.DMA((4,))],
        compiler_params=pltpu.CompilerParams(vmem_limit_bytes=16 * 1024 * 1024),
        cost_estimate=pl.CostEstimate(
            flops=16 * 512 * 4096, bytes_accessed=4 << 20, transcendentals=0
        ),
    )(cells.reshape(256, 1), jnp.asarray(unit, bf16))


def route(sphere_map):
    waves = sphere_map.shape[0]
    table = np.zeros((4, 32, 32), np.float32)
    table[:, :18, :18] = lookup_table().transpose(0, 2, 1)
    return pl.pallas_call(
        route_kernel,
        out_shape=jax.ShapeDtypeStruct((8, waves), jnp.int32),
        compiler_params=pltpu.CompilerParams(vmem_limit_bytes=8 * 1024 * 1024),
        cost_estimate=pl.CostEstimate(
            flops=2 * 128 * 32 * waves, bytes_accessed=40 * waves, transcendentals=0
        ),
    )(sphere_map.reshape(1, waves), jnp.asarray(table.reshape(128, 32), bf16))


def pair_kernel(
    first_ref,
    second_ref,
    con_ref,
    table_ref,
    turn_ref,
    pair_ref,
    part_ref,
    wide_ref,
    val_ref,
    buffer_ref,
    sem_ref,
):
    copy = pltpu.make_async_copy(table_ref, buffer_ref, sem_ref)
    copy.start()
    for band in range(2):
        for x in range(4):
            start = (band * 4 + x) * 64
            wide_ref[start : start + 64, :] = first_ref[band, x].astype(f32)
            wide_ref[512 + start : 576 + start, :] = second_ref[band, x].astype(f32)
    left = lax.broadcasted_iota(jnp.int32, (4, 128), 1) < 64

    for y in range(0, LENGTH, 2):
        lanes = slice(y * 64, y * 64 + 128)
        for x in range(4):
            even = wide_ref[pl.ds(x * 64 + y, 4, stride=256), :]
            odd = wide_ref[pl.ds(x * 64 + y + 1, 4, stride=256), :]
            val_ref[2 * x, :, lanes] = jnp.where(left, even, pltpu.roll(odd, 64, 1))
            val_ref[2 * x + 1, :, lanes] = jnp.where(left, pltpu.roll(even, 64, 1), odd)

    chunk = 512

    @pl.loop(0, LENGTH * LENGTH // chunk)
    def _(k):
        lanes = pl.ds(pl.multiple_of(k * chunk, chunk), chunk)
        for x in range(4):
            con_re = con_ref[2 * x, :, lanes].astype(f32)
            con_im = con_ref[2 * x + 1, :, lanes].astype(f32)
            for v in range(4):
                val_re = val_ref[2 * x, pl.ds(v, 1), lanes]
                val_im = val_ref[2 * x + 1, pl.ds(v, 1), lanes]
                real = val_re * con_re + val_im * con_im
                imag = val_re * con_im - val_im * con_re
                pair_ref[pl.ds(x * 128 + v * 16, 16), lanes] = real.astype(bf16)
                pair_ref[pl.ds(x * 128 + 64 + v * 16, 16), lanes] = imag.astype(bf16)

    copy.wait()
    total = jnp.zeros(part_ref.shape, f32)
    for x in range(4):
        mixed = lax.dot_general(
            buffer_ref[...],
            pair_ref[x * 128 : (x + 1) * 128, :],
            (((1,), (1,)), ((), ())),
            preferred_element_type=f32,
        )
        value = mixed[:256] + swap(mixed[256:])
        total += turn_ref[:, x : x + 1] * value
        total += swap(turn_ref[:, 4 + x : 5 + x] * value)
    part_ref[...] = total


def pair_call(first, second, con, table, turn):
    whole = pl.BlockSpec(memory_space=pltpu.VMEM)
    table = pltpu.with_memory_space_constraint(table, pltpu.HBM)
    return pl.pallas_call(
        pair_kernel,
        in_specs=[whole] * 3 + [pl.BlockSpec(memory_space=pltpu.HBM), whole],
        out_shape=[
            pltpu.VMEM((512, 4096), bf16),
            jax.ShapeDtypeStruct((256, 128), f32),
        ],
        scratch_shapes=[
            pltpu.VMEM((1024, 128), f32),
            pltpu.VMEM((8, 4, 4096), f32),
            pltpu.VMEM((512, 4096), bf16),
            pltpu.SemaphoreType.DMA,
        ],
        compiler_params=pltpu.CompilerParams(vmem_limit_bytes=22 * 1024 * 1024),
        cost_estimate=pl.CostEstimate(
            flops=2 * 512 * 512 * 4096, bytes_accessed=10 << 20, transcendentals=0
        ),
    )(first, second, con, table, turn)


def plane_kernel(pair_ref, table_ref, send_ref, buffer_ref, sem_ref):
    copies = [
        pltpu.make_async_copy(
            table_ref.at[pl.ds(i * 256, 256)], buffer_ref.at[i], sem_ref.at[i]
        )
        for i in range(4)
    ]
    for copy in copies:
        copy.start()
    for i in range(4):
        copies[i].wait()
        mixed = lax.dot_general(
            buffer_ref[i], pair_ref[...], (((1,), (1,)), ((), ())), preferred_element_type=f32
        )
        for x in range(4):
            part = mixed[:, x * 128 : (x + 1) * 128]
            cc, cs, sc, ss = (part[64 * k : 64 * (k + 1)] for k in range(4))
            sc, cs = swap(sc), swap(cs)
            same, other = cc - ss, cc + ss
            total, apart = sc + cs, sc - cs
            signs = (same + total, other + apart, other - apart, same - total)
            columns = jnp.concatenate([value.astype(bf16) for value in signs], axis=0)
            send_ref[:, 4 * i : 4 * i + 4, x] = columns.reshape(4, 4, SLOTS, 128)


def plane_call(pairs, table):
    return pl.pallas_call(
        plane_kernel,
        in_specs=[
            pl.BlockSpec(memory_space=pltpu.VMEM),
            pl.BlockSpec(memory_space=pltpu.HBM),
        ],
        out_shape=jax.ShapeDtypeStruct((4, GROUPS, 4, SLOTS, 128), bf16),
        scratch_shapes=[pltpu.VMEM((4, 256, 4096), bf16), pltpu.SemaphoreType.DMA((4,))],
        compiler_params=pltpu.CompilerParams(vmem_limit_bytes=24 * 1024 * 1024),
        cost_estimate=pl.CostEstimate(
            flops=2 * 1024 * 512 * 4096, bytes_accessed=8 << 20, transcendentals=0
        ),
    )(pairs, pltpu.with_memory_space_constraint(table, pltpu.HBM))


def line_kernel(
    me_ref,
    grid_ref,
    line8_ref,
    line16_ref,
    line24_ref,
    window_ref,
    weight_ref,
    out_ref,
    wide_ref,
    rho_ref,
    left_ref,
):
    lines = {8: line8_ref, 16: line16_ref, 24: line24_ref}

    @pl.loop(0, 4 * LENGTH, step=4)
    def _(x):
        for i in range(4):
            start = pl.multiple_of((x + i) * SLOTS, SLOTS)
            wide_ref[pl.ds(start, SLOTS), :] = grid_ref[x + i].astype(f32)

    last = BASE[-1] + 2 * HEIGHT[-1] + 1
    rho_ref[last - last % 8 :, :] = jnp.zeros((ROWS - last + last % 8, 512), f32)
    for slot in range(USED):
        lane_tiles = [
            wide_ref[pl.ds(q * LENGTH * SLOTS + slot, LENGTH, stride=SLOTS), :] for q in range(4)
        ]
        values = jnp.concatenate(lane_tiles, axis=1).astype(bf16)
        count, base = HEIGHT[slot] + 1, BASE[slot]
        rows = -(-count // 8) * 8
        mixed = jnp.dot(lines[rows][...], values, preferred_element_type=f32)
        for q in range(4):
            lanes = slice(q * 128, (q + 1) * 128)
            cosine, sine = mixed[:rows, lanes], swap(mixed[rows:, lanes])
            rho_ref[base + count - 1 : base + 2 * count - 1, lanes] = (cosine - sine)[:count]
            rho_ref[base : base + count, lanes] = (cosine + sine)[:count]

    me = me_ref[0]
    wave = lax.broadcasted_iota(jnp.int32, (256, 1024), 0)
    column = lax.broadcasted_iota(jnp.int32, (256, 1024), 1)
    for q in range(4):
        lanes = slice(q * 128, (q + 1) * 128)
        place = ((q * 16 + wave // 16) ^ me) * 16 + wave % 16
        order = jnp.where(column == place, 1.0, 0.0).astype(bf16)
        values = jnp.dot(order, window_ref[...], preferred_element_type=f32)
        scaled = (weight_ref[:, lanes] * values).astype(bf16).astype(f32)
        turned = -swap(scaled)
        for b in range(COL_DEV):
            left_ref[b * 32 : b * 32 + 16, lanes] = scaled[b * 16 : b * 16 + 16].astype(bf16)
            left_ref[b * 32 + 16 : b * 32 + 32, lanes] = turned[b * 16 : b * 16 + 16].astype(bf16)
    for n in range(0, ROWS, 128):
        product = lax.dot_general(
            left_ref[...],
            rho_ref[n : n + 128, :].astype(bf16),
            (((1,), (1,)), ((), ())),
            preferred_element_type=f32,
        )
        out_ref[:, n : n + 128] = product.astype(bf16)


def line_call(me, grid, lines, window, weight):
    whole = pl.BlockSpec(memory_space=pltpu.VMEM)
    return pl.pallas_call(
        line_kernel,
        in_specs=[pl.BlockSpec(memory_space=pltpu.SMEM)] + [whole] * 6,
        out_shape=jax.ShapeDtypeStruct((512, ROWS), bf16),
        scratch_shapes=[
            pltpu.VMEM((4 * LENGTH * SLOTS, 128), f32),
            pltpu.VMEM((ROWS, 512), f32),
            pltpu.VMEM((512, 512), bf16),
        ],
        compiler_params=pltpu.CompilerParams(vmem_limit_bytes=16 * 1024 * 1024),
        cost_estimate=pl.CostEstimate(
            flops=2 * 512 * 512 * ROWS, bytes_accessed=3 << 20, transcendentals=0
        ),
    )(me.reshape(1), grid, *lines, window, weight)


def split(value):
    high = value.astype(bf16)
    return high, (value - high.astype(f32)).astype(bf16)


def pick_kernel(parts_ref, rows_ref, out_ref, both_ref):
    for q in range(4):
        lanes = slice(q * ROWS, (q + 1) * ROWS)
        total = parts_ref[q].astype(f32)
        for y in range(1, 4):
            total += parts_ref[4 * y + q].astype(f32)
        both_ref[:32, lanes], both_ref[32:, lanes] = split(total)
    for n in range(0, 16 * CAP, 256):
        cell = lax.broadcasted_iota(jnp.int32, (CELLS, 256), 0)
        chosen = jnp.where(cell == rows_ref[:, n : n + 256], 1.0, 0.0).astype(bf16)
        found = jnp.dot(both_ref[...], chosen, preferred_element_type=f32)
        found = found[:32] + found[32:]
        for i in range(256 // CAP):
            out_ref[n // CAP + i] = found[:, i * CAP : (i + 1) * CAP]


def pick_call(parts, rows):
    return pl.pallas_call(
        pick_kernel,
        out_shape=jax.ShapeDtypeStruct((16, 32, CAP), f32),
        scratch_shapes=[pltpu.VMEM((64, CELLS), bf16)],
        compiler_params=pltpu.CompilerParams(vmem_limit_bytes=16 * 1024 * 1024),
        cost_estimate=pl.CostEstimate(
            flops=2 * 64 * CELLS * 16 * CAP, bytes_accessed=2 << 20, transcendentals=0
        ),
    )(parts, rows)


def place_kernel(found_ref, place_ref, out_ref, both_ref):
    for i in range(16):
        both_ref[:32, i * CAP : (i + 1) * CAP], both_ref[32:, i * CAP : (i + 1) * CAP] = split(
            found_ref[i]
        )
    for n in range(0, out_ref.shape[1], 256):
        slot = lax.broadcasted_iota(jnp.int32, (16 * CAP, 256), 0)
        chosen = jnp.where(slot == place_ref[:, n : n + 256], 1.0, 0.0).astype(bf16)
        value = jnp.dot(both_ref[...], chosen, preferred_element_type=f32)
        out_ref[:, n : n + 256] = value[:32] + value[32:]


def place_call(found, place):
    return pl.pallas_call(
        place_kernel,
        out_shape=jax.ShapeDtypeStruct((32, place.shape[1]), f32),
        scratch_shapes=[pltpu.VMEM((64, 16 * CAP), bf16)],
        compiler_params=pltpu.CompilerParams(vmem_limit_bytes=16 * 1024 * 1024),
        cost_estimate=pl.CostEstimate(
            flops=2 * 64 * 16 * CAP * 1280, bytes_accessed=1 << 20, transcendentals=0
        ),
    )(found, place)


def block(value, index):
    return lax.dynamic_index_in_dim(value, index, 0, keepdims=False)


def far(value, axis, step):
    size = math.prod(AXES[name] for name in (axis if isinstance(axis, tuple) else (axis,)))
    return lax.ppermute(value, axis, [(i, i ^ step) for i in range(size)])


def scatter_inputs(store, con, slot_index, sphere_map):
    y, zl, c = (lax.axis_index(name) for name in BAND)
    from_y, from_zl, from_c = slot_index // 4, slot_index // 2 % 2, slot_index % 2
    other = far(block(store, 1 - c), "c", 1)
    held = jnp.where(c == from_c, block(store, c), other)

    def along_rows(value):
        sent = [block(value, y ^ step) for step in range(1, 4)]
        got = [far(sent[step - 1], "y", step) for step in range(1, 4)]
        mine = block(value, y)
        for step in range(1, 4):
            mine = jnp.where(y ^ from_y == step, got[step - 1], mine)
        return mine, sent

    def along_pairs(value):
        return jnp.where(zl == from_zl, block(value, zl), far(block(value, 1 - zl), "zl", 1))

    later = held[:, :, 2:].swapaxes(0, 1)
    first, sent = along_rows(held[:, :, :2])
    con = lax.optimization_barrier((con, sent, block(later, 1 - zl)))[0]
    rows = jnp.stack([con] + [far(con, "y", step) for step in range(1, 4)])
    sphere_map = lax.optimization_barrier((sphere_map, rows))[0]
    pairs = jnp.stack([rows, far(rows, "zl", 1)], axis=1)
    both = jnp.stack([pairs, far(pairs, "c", 1)], axis=2)
    first = along_pairs(first)
    second = along_rows(along_pairs(later))[0]
    return first, second, both.reshape((16,) + con.shape), sphere_map


def window_and_planes(pairs, part, table):
    x = lax.axis_index("x")
    part = part.reshape(4, 4, 16, 128)
    got = [block(part, x)] + [far(block(part, x ^ step), "x", step) for step in range(1, 4)]
    planes = plane_call(pairs, table)
    got, planes = lax.optimization_barrier((got, planes))
    total = got[0] + got[1] + got[2] + got[3]
    got = [far(total, "zh", step) for step in range(1, 4)]
    got[0], planes = lax.optimization_barrier((got[0], planes))
    return (total + got[0] + got[1] + got[2]).astype(bf16), planes


def gather_window(value):
    value = jnp.stack([value] + [far(value, "x", step) for step in range(1, 4)])
    return jnp.stack([value] + [far(value, ("zl", "c"), step) for step in range(1, 4)])


def on_device(valence_store, valence_energy, conduction, conduction_energy, sphere_map, owner):
    band_count, fft_count = lax.axis_size(BAND), lax.axis_size(FFT)
    me_band, me_fft, me_near = (lax.axis_index(axis) for axis in (BAND, FFT, NEAR))
    valence_total = valence_store.shape[1]
    conduction_total = conduction.shape[0] * band_count
    window_total = COL_DEV * band_count
    share = valence_total // band_count
    waves = sphere_map.shape[0] // fft_count

    con = conduction.reshape(4, 64, 2, 64).transpose(0, 2, 1, 3).reshape(8, 4096)
    energy, pieces = conduction_energy[0], []
    for _ in range(3):
        pieces.append(lax.reduce_precision(energy, 8, 7))
        energy = energy - pieces[-1]
    extra = jnp.zeros((8, 128), f32).at[0, :3].set(jnp.stack(pieces)).astype(bf16)
    con = jnp.concatenate([con, extra], axis=1)
    store = valence_store.reshape((2, 4, 2, share) + valence_store.shape[2:])
    slot_index = owner[0] % band_count
    first, second, con, sphere_map = scatter_inputs(store, con, slot_index, sphere_map)
    energies = jnp.sum(con[:, 0, 4096:4099].astype(f32), axis=1)
    con = con[:, :, :4096].transpose(1, 0, 2)

    window_cells = sphere_map[:window_total]
    window_table = window_call(window_cells)
    kx = (window_cells // 4096)[:, None]
    x_here = 4 * me_fft + jnp.arange(4, dtype=jnp.int32)
    angle = 2.0 * math.pi / 64 * ((kx * x_here[None]) % 64).astype(f32)
    turn = jnp.concatenate([jnp.cos(angle) / 8.0, jnp.sin(angle) / 8.0], axis=1)
    turn = turn.astype(bf16).astype(f32)

    pairs, part = pair_call(first, second, con, window_table, turn)
    part, planes = window_and_planes(pairs, part, jnp.asarray(plane_table()))
    window = gather_window(part)
    sphere_map = lax.optimization_barrier((sphere_map, planes))[0]

    routed = route(sphere_map)
    by_block = routed[0].reshape(fft_count, waves)
    devices = jnp.arange(fft_count, dtype=jnp.int32)
    counts = jnp.sum(
        (by_block[:, None, :] == devices[None, :, None]).astype(jnp.int32), axis=2
    )
    fits = jnp.all(routed[2] == 1) & jnp.all(counts <= CAP)
    mine = by_block == me_fft
    own_block = lax.dynamic_index_in_dim(by_block, me_fft, 0, keepdims=False)
    from_device = own_block[None] == devices[:, None]
    masks = jnp.concatenate([mine, from_device], axis=0).astype(bf16)
    before = lax.broadcasted_iota(jnp.int32, (waves, waves), 0)
    upto = lax.broadcasted_iota(jnp.int32, (waves, waves), 1)
    order = jnp.dot(masks, (before <= upto).astype(bf16), preferred_element_type=f32)
    order = order.astype(jnp.int32) - 1
    slots = jnp.arange(CAP, dtype=jnp.int32)
    chosen = mine[:, :, None] & (order[:fft_count, :, None] == slots)
    row_block = routed[1].reshape(fft_count, waves)
    halves = jnp.stack([row_block // 64, row_block % 64], axis=1).astype(bf16)
    listed = jnp.einsum(
        "fpg,fgs->fps", halves, chosen.astype(bf16), preferred_element_type=f32
    ).astype(jnp.int32)
    rows = (listed[:, 0] * 64 + listed[:, 1]).reshape(1, fft_count * CAP)
    rank = jnp.sum(jnp.where(from_device, order[fft_count:], 0), axis=0)
    place = (own_block * CAP + rank).reshape(1, waves)
    grid = lax.all_to_all(planes.reshape(64, 4, SLOTS, 128), NEAR, 0, 0, tiled=True)
    norm_scale = 1.0 / math.sqrt(valence_total * conduction_total)
    near = jnp.arange(4, dtype=jnp.int32)
    bands = (near % 2) * 8 + lax.axis_index("y") * 2 + near // 2
    hot = bands[:, None, None] == (jnp.arange(valence_total) // share)[None, None, :]
    hot = hot & (jnp.arange(share)[None, :, None] == (jnp.arange(valence_total) % share))
    near_valence = jnp.sum(jnp.where(hot, valence_energy, 0.0), axis=2)
    steps = jnp.arange(band_count, dtype=jnp.int32)
    places = (near ^ (me_band % 4))[:, None] ^ steps[None, :]
    near_conduction = jnp.sum(
        jnp.where(places[:, :, None] == steps[None, None, :], energies, 0.0), axis=2
    )
    weight = 4.0 * norm_scale / (near_valence[:, :, None] - near_conduction[:, None, :])
    weight = jnp.broadcast_to(weight.reshape(4, 1, 64), (4, 2, 64)).reshape(1, 512)

    lines = [jnp.asarray(table) for table in line_tables()]
    grid, window = grid.reshape(256, SLOTS, 128), window.reshape(1024, 128)
    partial = line_call(me_near - me_near % 4, grid, lines, window, weight)
    parts = lax.all_to_all(partial.reshape(band_count, 32, ROWS), BAND, 0, 0, tiled=True)
    found = pick_call(parts, rows)
    found = lax.all_to_all(found, FFT, 0, 0, tiled=True)
    result = place_call(found, place).reshape(2, COL_DEV, waves)
    args = (valence_store, valence_energy, conduction, conduction_energy, sphere_map, owner)
    return lax.cond(fits, lambda *_: result, general_path, *args)


def broadcast(value, axis, source):
    kept = jnp.where(lax.axis_index(axis) == source, value, 0).astype(value.dtype)
    return lax.psum(kept, axis)


def dft_table(length):
    steps_n = lax.broadcasted_iota(jnp.int32, (length, length), 0)
    steps_k = lax.broadcasted_iota(jnp.int32, (length, length), 1)
    phase_angle = 2.0 * math.pi / length * (steps_n * steps_k % length).astype(jnp.float32)
    factor = 1.0 / math.sqrt(length)
    cosine = jnp.cos(phase_angle) * factor
    sine_part = jnp.sin(phase_angle) * factor
    upper_half = jnp.stack([cosine, -sine_part], axis=1)
    lower_half = jnp.stack([sine_part, cosine], axis=1)
    return jnp.stack([upper_half, lower_half], axis=0).astype(jnp.bfloat16)


def pair_products(valence, conduction):
    length = valence.shape[-1] // 2
    val_re = valence[..., :length].astype(jnp.float32)[:, None]
    val_im = valence[..., length:].astype(jnp.float32)[:, None]
    con_re = conduction[..., :length].astype(jnp.float32)[None]
    con_im = conduction[..., length:].astype(jnp.float32)[None]
    real_part = val_re * con_re + val_im * con_im
    imag_part = val_re * con_im - val_im * con_re
    joined = jnp.concatenate([real_part, imag_part], axis=-1).astype(jnp.bfloat16)
    return joined.reshape((-1,) + joined.shape[2:])


def along_z(values_in, twiddle):
    length = twiddle.shape[1]
    square = twiddle.reshape(2 * length, 2 * length)
    return jnp.dot(values_in, square, preferred_element_type=jnp.float32).astype(jnp.bfloat16)


def along_y(values_in, twiddle):
    length = twiddle.shape[1]
    split = values_in.reshape(values_in.shape[:3] + (2, length))
    mixed = jnp.einsum("axypz,pyqk->axkqz", split, twiddle, preferred_element_type=jnp.float32)
    return mixed.reshape(values_in.shape).astype(jnp.bfloat16)


def along_x(values_in, twiddle):
    length = twiddle.shape[1]
    split = values_in.reshape(values_in.shape[:3] + (2, length))
    mixed = jnp.einsum("axypz,pxqk->aqkyz", split, twiddle, preferred_element_type=jnp.float32)
    return mixed.astype(jnp.bfloat16)


def window_matrix(window, weights):
    scaled_re = (weights[:, None] * window[:, 0, :].astype(jnp.float32)).T
    scaled_im = (weights[:, None] * window[:, 1, :].astype(jnp.float32)).T
    first_row = jnp.stack([scaled_re, scaled_im], axis=2)
    second_row = jnp.stack([-scaled_im, scaled_re], axis=2)
    joined = jnp.stack([first_row, second_row], axis=0).astype(jnp.bfloat16)
    return joined.reshape(2 * joined.shape[1], 2 * joined.shape[2])


def general_path(valence_store, valence_energy, conduction, conduction_energy, sphere_map, owner):
    band_count = lax.axis_size(BAND)
    conduction_dev = conduction.shape[0]
    valence_total = valence_store.shape[1]
    length = conduction.shape[2]
    norm_scale = 1.0 / math.sqrt(valence_total * conduction_dev * band_count)
    twiddle = dft_table(length)
    window_total = COL_DEV * band_count
    slot_index = owner[0] % band_count
    valence = broadcast(valence_store, BAND, slot_index)[0]
    pair_grid = along_y(along_z(pair_products(valence, conduction), twiddle), twiddle)
    weights = (4.0 * norm_scale / (valence_energy[:, None] - conduction_energy[None, :])).reshape(
        -1
    )
    whole_grids = lax.all_to_all(pair_grid, FFT, split_axis=0, concat_axis=1, tiled=True)
    spectrum = along_x(whole_grids, twiddle)
    flat_grid = spectrum.reshape(spectrum.shape[0], 2, -1)
    sphere = jnp.take(flat_grid, sphere_map, axis=2)
    row_block = lax.all_to_all(sphere, FFT, split_axis=2, concat_axis=0, tiled=True)
    window = lax.all_gather(sphere[:, :, :window_total], FFT, axis=0, tiled=True)
    left_side = window_matrix(window, weights)
    right_side = row_block.reshape(-1, row_block.shape[2])
    product = jnp.dot(left_side, right_side, preferred_element_type=jnp.float32)
    partial_value = product.reshape(2, window_total, -1)
    return lax.psum_scatter(partial_value, BAND, scatter_dimension=1, tiled=True)


def solution(mesh):
    placed = (
        P(BAND, None, FFT, None, None),
        P(),
        P(BAND, FFT, None, None),
        P(BAND),
        P(),
        P(),
    )
    fine = Mesh(mesh.devices.reshape(tuple(AXES.values())), tuple(AXES))
    return jax.shard_map(
        on_device, mesh=fine, in_specs=placed, out_specs=P(None, BAND, FFT), check_vma=False
    )
```
